32 devices in a mesh: dp: 4 (over y, x), ctx: 4 (over z), wt: 2 (over core).
Axes of the slice: x: 2, y: 2, z: 4, core: 2. Of those that a mesh axis runs over, the one named last changes fastest.
Arguments:
- hidden: bfloat16 [8, 1024, 1088], P('dp', ('ctx', 'wt')), may hold values from -6 to 6
- block_order: int32 [8], replicated, may hold values from 0 to 7, as said below
- ln1_gain: bfloat16 [1088], replicated, may hold values from 0.5 to 1.5
- ln1_bias: bfloat16 [1088], replicated, may hold values from -1.796875 to 1.796875
- w_qkv: bfloat16 [1088, 3264], P('wt'), may hold values from -0.1875 to 0.1875
- q_bias: bfloat16 [1088], replicated, may hold values from -3 to 3
- v_bias: bfloat16 [1088], replicated, may hold values from -0.59765625 to 0.59765625
- w_proj: bfloat16 [1088, 1088], P('wt'), may hold values from -0.75 to 0.75
- proj_bias: bfloat16 [1088], replicated, may hold values from -1.796875 to 1.796875
- ln2_gain: bfloat16 [1088], replicated, may hold values from 0.5 to 1.5
- ln2_bias: bfloat16 [1088], replicated, may hold values from -1.796875 to 1.796875
- w_up: bfloat16 [1088, 4352], P(None, 'wt'), may hold values from -0.1875 to 0.1875
- up_bias: bfloat16 [4352], P('wt'), may hold values from -3 to 3
- w_down: bfloat16 [4352, 1088], P('wt'), may hold values from -0.09375 to 0.09375
- down_bias: bfloat16 [1088], replicated, may hold values from -1.796875 to 1.796875
- cotangent: bfloat16 [8, 1024, 1088], P('dp', ('ctx', 'wt')), may hold values from -6 to 6
Outputs:
- output: bfloat16 [8, 1024, 1088], P('dp', ('ctx', 'wt'))
- grad_hidden: bfloat16 [8, 1024, 1088], P('dp', ('ctx', 'wt'))
- grad_ln1_gain: float32 [1088], P('wt')
- grad_ln1_bias: float32 [1088], P('wt')
- grad_w_qkv: float32 [1088, 3264], P('wt')
- grad_q_bias: float32 [1088], P('wt')
- grad_v_bias: float32 [1088], P('wt')
- grad_w_proj: float32 [1088, 1088], P('wt')
- grad_proj_bias: float32 [1088], P('wt')
- grad_ln2_gain: float32 [1088], P('wt')
- grad_ln2_bias: float32 [1088], P('wt')
- grad_w_up: float32 [1088, 4352], P(None, 'wt')
- grad_up_bias: float32 [4352], P('wt')
- grad_w_down: float32 [4352, 1088], P('wt')
- grad_down_bias: float32 [1088], P('wt')
The draws below stay inside these ranges and needn't reach their ends.
Inputs may be any that keep to these rules, and one draw needn't show every extreme that they name: `block_order`: entries 2 r and 2 r + 1 are the causal blocks stored at cycle position r: every block number appears once, and the two of one cycle position add up to 7.
All inputs are finite; a program needn't handle non-finite values.
Results may differ from the reference program's by a relative error of at most 0.019.
Values may be sent and summed in bfloat16 or wider, within the bound.
No kernel may reach another device: no remote copies, remote signals or barrier semaphores. Data moves between devices by JAX's collectives and lax.ppermute only.
A program may use at most 320 MiB of HBM per device.

```python
import math
import jax
import jax.numpy as jnp
from jax import lax

D = 1088
HEADS = 17
HEAD = 64
FF = 4352
SEQS = 8
LEN = 1024
BLOCKS = 8


def draw_block_order(key, part):
    key = jax.random.fold_in(key, 11)
    first_key, latter_random_seed = jax.random.split(key)
    earlier = jax.random.permutation(first_key, BLOCKS // 2)
    flip_bits = jax.random.randint(latter_random_seed, (BLOCKS // 2,), 0, 2)
    leading = jnp.where(flip_bits == 1, earlier, BLOCKS - 1 - earlier)
    trailing = BLOCKS - 1 - leading
    return jnp.stack([leading, trailing], axis=1).reshape(BLOCKS).astype(jnp.int32)


def block_levels(own_key, extent, cuts, least, largest):
    def one(axis_at, blocks):
        steps = jax.random.uniform(jax.random.fold_in(jax.random.fold_in(own_key, 6), axis_at), (blocks,), jnp.float32, least / len(cuts), largest / len(cuts))
        return jnp.repeat(jnp.exp(steps), extent[axis_at] // blocks).reshape((-1,) + (1,) * (len(extent) - axis_at - 1))

    level = one(*cuts[0])
    for cut in cuts[1:]:
        level = level * one(*cut)
    return level


def centred(own_key, dims, width, bound, cuts=(), held_as=jnp.bfloat16):
    values = width * jax.random.normal(own_key, dims, jnp.float32)
    if cuts:
        values = values * block_levels(own_key, dims, cuts, -0.22, 0.18)
    return jnp.clip(values, -bound, bound).astype(held_as)


def setup_inputs(seed: int = 0) -> dict:
    splits = jax.random.split(jax.random.key(seed), 17)
    hidden = centred(splits[0], (SEQS, LEN, D), 1.0, 6.0, ((0, 4), (1, 8)))
    block_order = draw_block_order(jax.random.fold_in(splits[16], 71), 0)
    ln1_gain = jnp.clip(1.0 + 0.1 * jax.random.normal(splits[2], (D,), jnp.float32), 0.5, 1.5).astype(jnp.bfloat16)
    ln1_bias = centred(splits[3], (D,), 0.3, 1.796875)
    w_qkv = centred(splits[4], (D, 3 * D), D ** -0.5, 0.1875, ((0, 2),))
    q_bias = centred(splits[5], (D,), 0.5, 3.0)
    v_bias = centred(splits[6], (D,), 0.1, 0.59765625)
    w_proj = centred(splits[7], (D, D), (D // 16) ** -0.5, 0.75, ((0, 2),))
    proj_bias = centred(splits[8], (D,), 0.3, 1.796875)
    ln2_gain = jnp.clip(1.0 + 0.1 * jax.random.normal(splits[9], (D,), jnp.float32), 0.5, 1.5).astype(jnp.bfloat16)
    ln2_bias = centred(splits[10], (D,), 0.3, 1.796875)
    w_up = centred(splits[11], (D, FF), D ** -0.5, 0.1875, ((1, 2),))
    up_bias = centred(splits[12], (FF,), 0.5, 3.0, ((0, 2),))
    w_down = centred(splits[13], (FF, D), FF ** -0.5, 0.09375, ((0, 2),))
    down_bias = centred(splits[14], (D,), 0.3, 1.796875)
    cotangent = centred(splits[15], (SEQS, LEN, D), 1.0, 6.0, ((0, 4), (1, 8)))
    return dict(hidden=hidden, block_order=block_order, ln1_gain=ln1_gain, ln1_bias=ln1_bias, w_qkv=w_qkv, q_bias=q_bias, v_bias=v_bias, w_proj=w_proj, proj_bias=proj_bias, ln2_gain=ln2_gain, ln2_bias=ln2_bias, w_up=w_up, up_bias=up_bias, w_down=w_down, down_bias=down_bias, cotangent=cotangent)


@jax.custom_vjp
def low(v):
    return lax.optimization_barrier(v.astype(jnp.bfloat16)).astype(jnp.float32)

@jax.custom_vjp
def low_back(v):
    return v

def low_keep(v):
    return (low(v), None)

def low_pass(kept, grad):
    return (grad,)

def back_keep(v):
    return (v, None)

def back_low(kept, grad):
    return (low(grad),)
low.defvjp(low_keep, low_pass)
low_back.defvjp(back_keep, back_low)
epsilon = 1e-05
highest = lax.Precision.HIGHEST

def layer_norm(values, gain, offset):
    average = lax.optimization_barrier(jnp.mean(values, axis=-1, keepdims=True))
    mean_shifted_input = values - average
    variance = lax.optimization_barrier(jnp.mean(mean_shifted_input * mean_shifted_input, axis=-1, keepdims=True))
    return mean_shifted_input * lax.rsqrt(variance + epsilon) * gain + offset

def row_places(block_order):
    block_rows = LEN // BLOCKS
    row_index = jnp.arange(LEN, dtype=jnp.int32)
    slots = jnp.arange(BLOCKS, dtype=jnp.int32)
    owner_rank = lax.optimization_barrier(jnp.sum(jnp.where((row_index // block_rows)[:, None] == slots[None, :], block_order[None, :], 0), axis=1)).astype(jnp.int32)
    return (owner_rank * block_rows + row_index % block_rows).astype(jnp.int32)

def attend_rows(query_rows, query_places, keys, values, slot_indices):
    scores = low_back(jnp.einsum('qhe,khe->hqk', query_rows, keys, precision=highest))
    visible = slot_indices[None, None, :] <= query_places[None, :, None]
    probs = low(jax.nn.softmax(jnp.where(visible, scores, -jnp.inf), axis=-1))
    return jnp.einsum('hqk,khe->qhe', probs, values, precision=highest)

def attention(query, keys, values, slot_indices):
    query_block = math.gcd(LEN, 512)
    block_count = LEN // query_block
    query_blocks = query.reshape(block_count, query_block, HEADS, HEAD)
    place_blocks = slot_indices.reshape(block_count, query_block)
    one_block = jax.checkpoint(lambda operands: attend_rows(operands[0], operands[1], keys, values, slot_indices))
    return lax.map(one_block, (query_blocks, place_blocks)).reshape(LEN, D)

def layer(inputs, slot_indices, params):
    gain_one, bias_one, triple_weight_matrix, query_bias, value_bias, proj_matrix, proj_offset, gain_two, bias_two, up_matrix, up_offset, down_matrix, down_offset = params
    scale = 1.0 / math.sqrt(HEAD)
    normed = low(layer_norm(inputs, gain_one, bias_one))
    blended_rows = jnp.dot(normed, triple_weight_matrix, precision=highest)
    query = low(low_back((blended_rows[:, :D] + query_bias) * scale)).reshape(LEN, HEADS, HEAD)
    keys = low(low_back(blended_rows[:, D:2 * D])).reshape(LEN, HEADS, HEAD)
    values = low(low_back(blended_rows[:, 2 * D:] + value_bias)).reshape(LEN, HEADS, HEAD)
    attended = low(low_back(attention(query, keys, values, slot_indices)))
    middle = inputs + low_back(jnp.dot(attended, proj_matrix, precision=highest) + proj_offset)
    normed_two = low(layer_norm(middle, gain_two, bias_two))
    pre_act = low_back(jnp.dot(normed_two, up_matrix, precision=highest) + up_offset)
    activated = low(jax.nn.gelu(pre_act, approximate=True))
    return middle + jnp.dot(activated, down_matrix, precision=highest) + down_offset

def reference(hidden, block_order, ln1_gain, ln1_bias, w_qkv, q_bias, v_bias, w_proj, proj_bias, ln2_gain, ln2_bias, w_up, up_bias, w_down, down_bias, cotangent):
    slot_indices = row_places(block_order)
    params = tuple((weight.astype(jnp.float32) for weight in (ln1_gain, ln1_bias, w_qkv, q_bias, v_bias, w_proj, proj_bias, ln2_gain, ln2_bias, w_up, up_bias, w_down, down_bias)))

    def forward(inputs, weights):
        one_layer = jax.checkpoint(lambda sequence: layer(sequence, slot_indices, weights))
        return lax.map(one_layer, inputs)
    result, pullback = jax.vjp(forward, hidden.astype(jnp.float32), params)
    grad_inputs, grads = pullback(cotangent.astype(jnp.float32))
    return (result.astype(jnp.bfloat16), grad_inputs.astype(jnp.bfloat16), grads[0], grads[1], grads[2], grads[3], grads[4], grads[5], grads[6], grads[7], grads[8], grads[9], grads[10], grads[11], grads[12])
```

```python
import math

import jax
import jax.numpy as jnp
from jax import lax
from jax.experimental import pallas as pl
from jax.experimental.layout import Layout, with_layout_constraint
from jax.experimental.pallas import tpu as pltpu
from jax.sharding import PartitionSpec as P

HEADS = 17

epsilon = 1e-05
masked_value = -1e30
low_type = jnp.bfloat16
full_type = jnp.float32


def wide(array):
    return array.astype(full_type)


def layer_norm(values, gain, offset):
    average = jnp.mean(values, axis=-1, keepdims=True)
    shifted = values - average
    variance = jnp.mean(shifted * shifted, axis=-1, keepdims=True)
    return shifted * lax.rsqrt(variance + epsilon) * gain + offset


def gelu_tanh(values):
    return jax.nn.gelu(values, approximate=True)


def contract(first, second, first_dim, second_dim):
    return lax.dot_general(
        first, second, (((first_dim,), (second_dim,)), ((), ())), preferred_element_type=full_type
    )


def repeat(start, stop, body, carry):
    if isinstance(start, int) and isinstance(stop, int) and stop - start <= 4:
        for index in range(start, stop):
            carry = body(index, carry)
        return carry
    return lax.fori_loop(start, stop, body, carry)


def pair_of(ref, index):
    return jnp.concatenate([ref[2 * index], ref[2 * index + 1]], axis=-1)


def put_pair(ref, index, tile):
    half = tile.shape[-1] // 2
    ref[2 * index] = tile[:, :half].astype(ref.dtype)
    ref[2 * index + 1] = tile[:, half:].astype(ref.dtype)


def causal(scores):
    key_at = lax.broadcasted_iota(jnp.int32, scores.shape, 0)
    query_at = lax.broadcasted_iota(jnp.int32, scores.shape, 1)
    return jnp.where(key_at <= query_at, scores, masked_value)


def forward_kernel(ranks, mixed_ref, out_ref, lse_ref, queries, keys, values, outs):
    count = mixed_ref.shape[0]
    block = mixed_ref.shape[-1] // 2
    for piece in range(count):
        for half in range(2):
            rank = ranks[2 * piece + half]
            span = slice(half * block, (half + 1) * block)
            queries[rank] = mixed_ref[piece, 0, 0, :, span]
            keys[rank] = mixed_ref[piece, 1, 0, :, span]
            values[rank] = mixed_ref[piece, 2, 0, :, span]

    def query_tile(at, unused):
        query = pair_of(queries, at)

        def scores_at(key_at, diagonal=False):
            scores = contract(pair_of(keys, key_at), query, 0, 0)
            return causal(scores) if diagonal else scores

        def key_tile(key_at, carry, diagonal=False):
            highest, total, accum = carry
            scores = scores_at(key_at, diagonal)
            new_highest = jnp.maximum(highest, jnp.max(scores, axis=0, keepdims=True))
            probs = jnp.exp(scores - new_highest)
            shrink = jnp.exp(highest - new_highest)
            total = total * shrink + jnp.sum(probs, axis=0, keepdims=True)
            accum = accum * shrink + contract(
                pair_of(values, key_at), probs.astype(low_type), 1, 0
            )
            return new_highest, total, accum

        if isinstance(at, int):
            tiles = [scores_at(key_at, key_at == at) for key_at in range(at + 1)]
            highest = jnp.max(tiles[0], axis=0, keepdims=True)
            for tile in tiles[1:]:
                highest = jnp.maximum(highest, jnp.max(tile, axis=0, keepdims=True))
            total = jnp.zeros((1, 2 * block), full_type)
            accum = jnp.zeros(query.shape, full_type)
            for key_at, tile in enumerate(tiles):
                probs = jnp.exp(tile - highest)
                total = total + jnp.sum(probs, axis=0, keepdims=True)
                accum = accum + contract(pair_of(values, key_at), probs.astype(low_type), 1, 0)
        else:
            start = (
                jnp.full((1, 2 * block), masked_value, full_type),
                jnp.zeros((1, 2 * block), full_type),
                jnp.zeros(query.shape, full_type),
            )
            carry = lax.fori_loop(0, at, key_tile, start)
            highest, total, accum = key_tile(at, carry, True)
        put_pair(outs, at, accum / total)
        lse_ref[0, pl.ds(at, 1), :] = highest + jnp.log(total)
        return unused

    repeat(0, count, query_tile, 0)
    for piece in range(count):
        for half in range(2):
            rank = ranks[2 * piece + half]
            out_ref[piece, 0, :, half * block : (half + 1) * block] = outs[rank]


def backward_kernel(
    ranks,
    mixed_ref,
    out_ref,
    grad_ref,
    lse_ref,
    result_ref,
    queries,
    keys,
    values,
    outs,
    grads,
    query_grads,
    key_grads,
    value_grads,
    deltas,
):
    count = mixed_ref.shape[0]
    block = mixed_ref.shape[-1] // 2
    for piece in range(count):
        for half in range(2):
            rank = ranks[2 * piece + half]
            span = slice(half * block, (half + 1) * block)
            queries[rank] = mixed_ref[piece, 0, 0, :, span]
            keys[rank] = mixed_ref[piece, 1, 0, :, span]
            values[rank] = mixed_ref[piece, 2, 0, :, span]
            outs[rank] = out_ref[piece, 0, :, span]
            grads[rank] = grad_ref[piece, 0, :, span]

    def delta_tile(at, unused):
        terms = pair_of(outs, at).astype(full_type) * pair_of(grads, at).astype(full_type)
        deltas[pl.ds(at, 1), :] = jnp.sum(terms, axis=0, keepdims=True)
        zeros = jnp.zeros(query_grads.shape[1:], full_type)
        query_grads[2 * at] = zeros
        query_grads[2 * at + 1] = zeros
        return unused

    repeat(0, count, delta_tile, 0)

    def key_tile(key_at, unused):
        key = pair_of(keys, key_at)
        value = pair_of(values, key_at)

        def query_tile(at, carry, diagonal=False):
            key_grad, value_grad = carry
            query = pair_of(queries, at)
            grad = pair_of(grads, at)
            scores = contract(key, query, 0, 0)
            if diagonal:
                scores = causal(scores)
            probs = jnp.exp(scores - lse_ref[0, pl.ds(at, 1), :])
            grad_probs = contract(value, grad, 0, 0)
            grad_scores = (probs * (grad_probs - deltas[pl.ds(at, 1), :])).astype(low_type)
            value_grad = value_grad + contract(grad, probs.astype(low_type), 1, 1)
            key_grad = key_grad + contract(query, grad_scores, 1, 1)
            query_grad = contract(key, grad_scores, 1, 0)
            query_grads[2 * at] += query_grad[:, :block]
            query_grads[2 * at + 1] += query_grad[:, block:]
            return key_grad, value_grad

        start = (jnp.zeros(key.shape, full_type), jnp.zeros(key.shape, full_type))
        carry = query_tile(key_at, start, True)
        key_grad, value_grad = repeat(key_at + 1, count, query_tile, carry)
        put_pair(key_grads, key_at, key_grad)
        put_pair(value_grads, key_at, value_grad)
        return unused

    repeat(0, count, key_tile, 0)
    for piece in range(count):
        for half in range(2):
            rank = ranks[2 * piece + half]
            span = slice(half * block, (half + 1) * block)
            result_ref[piece, 0, 0, :, span] = query_grads[rank].astype(low_type)
            result_ref[piece, 1, 0, :, span] = key_grads[rank]
            result_ref[piece, 2, 0, :, span] = value_grads[rank]


def attention_forward(ranks, mixed):
    count, _, heads, depth, rows = mixed.shape
    blocks = (2 * count, depth, rows // 2)
    return pl.pallas_call(
        forward_kernel,
        out_shape=(
            jax.ShapeDtypeStruct((count, heads, depth, rows), low_type),
            jax.ShapeDtypeStruct((heads, count, rows), full_type),
        ),
        grid_spec=pltpu.PrefetchScalarGridSpec(
            num_scalar_prefetch=1,
            grid=(heads,),
            in_specs=[
                pl.BlockSpec((count, 3, 1, depth, rows), lambda head, _: (0, 0, head, 0, 0))
            ],
            out_specs=(
                pl.BlockSpec((count, 1, depth, rows), lambda head, _: (0, head, 0, 0)),
                pl.BlockSpec((1, count, rows), lambda head, _: (head, 0, 0)),
            ),
            scratch_shapes=[pltpu.VMEM(blocks, low_type) for _ in range(4)],
        ),
        compiler_params=pltpu.CompilerParams(vmem_limit_bytes=40 * 2**20),
        cost_estimate=pl.CostEstimate(flops=0, bytes_accessed=0, transcendentals=0),
    )(ranks, mixed)


def attention_backward(ranks, mixed, outs, grads, lse):
    count, _, heads, depth, rows = mixed.shape
    blocks = (2 * count, depth, rows // 2)
    three = pl.BlockSpec((count, 3, 1, depth, rows), lambda head, _: (0, 0, head, 0, 0))
    one = pl.BlockSpec((count, 1, depth, rows), lambda head, _: (0, head, 0, 0))
    return pl.pallas_call(
        backward_kernel,
        out_shape=jax.ShapeDtypeStruct(mixed.shape, low_type),
        grid_spec=pltpu.PrefetchScalarGridSpec(
            num_scalar_prefetch=1,
            grid=(heads,),
            in_specs=[
                three,
                one,
                one,
                pl.BlockSpec((1, count, rows), lambda head, _: (head, 0, 0)),
            ],
            out_specs=three,
            scratch_shapes=[pltpu.VMEM(blocks, low_type) for _ in range(5)]
            + [pltpu.VMEM(blocks, full_type)]
            + [pltpu.VMEM(blocks, low_type) for _ in range(2)]
            + [pltpu.VMEM((count, rows), full_type)],
        ),
        compiler_params=pltpu.CompilerParams(vmem_limit_bytes=40 * 2**20),
        cost_estimate=pl.CostEstimate(flops=0, bytes_accessed=0, transcendentals=0),
    )(ranks, mixed, outs, grads, lse)


def swapped(array):
    return lax.ppermute(array, "wt", [(0, 1), (1, 0)])


def part_of(array, index, size, axis=0):
    return lax.dynamic_slice_in_dim(array, index * size, size, axis)


def in_order(first, second, flip, axis):
    return jnp.where(
        flip, jnp.concatenate([second, first], axis), jnp.concatenate([first, second], axis)
    )


def scattered(send):
    count = lax.axis_size("ctx")
    place = lax.axis_index("ctx")
    pieces = []
    for shift in range(count):
        piece = lax.dynamic_index_in_dim(send, lax.rem(place + shift, count), 0, False)
        if shift:
            hops = [(one, (one + shift) % count) for one in range(count)]
            piece = lax.ppermute(piece, "ctx", hops)
        pieces.append(piece)
    return jnp.stack(pieces)


def returned(pieces, axis):
    count = lax.axis_size("ctx")
    place = lax.axis_index("ctx")
    size = pieces.shape[axis + 1]
    shape = list(pieces.shape[1:])
    shape[axis] = size * count
    result = jnp.zeros(shape, pieces.dtype)
    for shift in range(count):
        piece = pieces[shift]
        if shift:
            hops = [(one, (one - shift) % count) for one in range(count)]
            piece = lax.ppermute(piece, "ctx", hops)
        source = lax.rem(place + shift, count)
        result = lax.dynamic_update_slice_in_dim(result, piece, source * size, axis)
    return result


def dp_hops(bit):
    return [(one, one ^ (1 << bit)) for one in range(lax.axis_size("dp"))]


def reduced(array, order):
    index = lax.axis_index("dp")
    for bit in order:
        half = array.shape[0] // 2
        high = lax.rem(lax.div(index, 1 << bit), 2)
        kept = part_of(array, high, half)
        arrived = lax.ppermute(part_of(array, 1 - high, half), "dp", dp_hops(bit))
        array = (kept.astype(full_type) + arrived.astype(full_type)).astype(low_type)
    return array


def spread(array, order):
    index = lax.axis_index("dp")
    for bit in reversed(order):
        high = lax.rem(lax.div(index, 1 << bit), 2)
        arrived = lax.ppermute(array, "dp", dp_hops(bit))
        array = in_order(array, arrived, high == 1, 0)
    return array


def halves_of_all(array, axes):
    index = lax.axis_index("dp")
    half = array.shape[0] // 2
    forth = tuple(range(len(axes)))
    gathered = []
    for part, order in ((array[:half], forth), (array[half:], forth[::-1])):
        for bit in order:
            high = lax.rem(lax.div(index, 1 << bit), 2)
            arrived = lax.ppermute(part, "dp", dp_hops(bit))
            part = in_order(part, arrived, high == 1, axes[bit])
        gathered.append(part)
    return gathered


def joined(forth, back, bits):
    forth = forth.reshape((2,) * bits + (-1, forth.shape[1]))
    forth = jnp.transpose(forth, (*reversed(range(bits)), bits, bits + 1))
    return jnp.stack([forth, back.reshape(forth.shape)], axis=bits).reshape(-1, forth.shape[-1])


def row_major(array):
    return with_layout_constraint(array, Layout(major_to_minor=(0, 1)))


def tied(*arrays):
    return lax.optimization_barrier(arrays)


def small_total_over_group(array):
    for bit in range(int(math.log2(lax.axis_size("dp")))):
        array = array + lax.ppermute(array, "dp", dp_hops(bit))
    count = lax.axis_size("ctx")
    total = array
    for shift in range(1, count):
        hops = [(one, (one + shift) % count) for one in range(count)]
        total = total + lax.ppermute(array, "ctx", hops)
    return total


def local(
    hidden,
    block_order,
    ln1_gain,
    ln1_bias,
    w_qkv,
    q_bias,
    v_bias,
    w_proj,
    proj_bias,
    ln2_gain,
    ln2_bias,
    w_up,
    up_bias,
    w_down,
    down_bias,
    cotangent,
):
    seqs, seq_dev, width = hidden.shape
    depth = width // HEADS
    scale = 1.0 / math.sqrt(depth)
    count = lax.axis_size("ctx")
    place = lax.axis_index("ctx")
    core = lax.axis_index("wt")
    half_width = width // 2
    rows = 2 * seq_dev
    group = -(-HEADS // count)
    padded = group * count
    bits = int(math.log2(lax.axis_size("dp")))
    upward = tuple(range(bits))
    downward = tuple(reversed(upward))

    def by_sequence(array):
        mine = lax.dynamic_index_in_dim(array, core, 0, False)
        theirs = lax.dynamic_index_in_dim(array, 1 - core, 0, False)
        return jnp.concatenate([mine, swapped(theirs)], axis=0)

    def by_rows(array):
        mine = array[:seq_dev]
        arrived = swapped(array[seq_dev:])
        return in_order(mine[None], arrived[None], core == 1, 0)

    sources = lax.rem(place - jnp.arange(count, dtype=jnp.int32) + count, count)
    slots = jnp.stack([2 * sources + core, 2 * sources + 1 - core], axis=1).reshape(-1)
    ranks = block_order[slots]

    rows_low = by_sequence(hidden)
    other_qkv = swapped(w_qkv)
    other_proj = swapped(w_proj)
    grad_low = by_sequence(cotangent)
    grad_rows = jnp.concatenate([grad_low, swapped(grad_low)], axis=0)
    grad_rows_near = lax.ppermute(grad_rows, "dp", dp_hops(0))
    grad_act = contract(w_down, grad_rows, 1, 1)

    inputs = wide(rows_low)
    normed, norm_one_pull = jax.vjp(layer_norm, inputs, wide(ln1_gain), wide(ln1_bias))
    normed_low = normed.astype(low_type)
    normed_own = part_of(normed_low, core, half_width, 1)
    normed_other = part_of(normed_low, 1 - core, half_width, 1)
    mixed = contract(w_qkv, normed_own, 0, 1) + contract(other_qkv, normed_other, 0, 1)
    offsets = jnp.concatenate([wide(q_bias), jnp.zeros((width,), full_type), wide(v_bias)])
    scales = jnp.concatenate([jnp.full((width,), scale, full_type), jnp.ones((2 * width,), full_type)])
    mixed = ((mixed + offsets[:, None]) * scales[:, None]).astype(low_type)

    def own_half(array):
        return part_of(array, core, half_width, 1) + swapped(
            part_of(array, 1 - core, half_width, 1)
        )

    def to_heads(array):
        array = array.reshape(-1, HEADS, depth, rows)
        array = jnp.pad(array, ((0, 0), (0, padded - HEADS), (0, 0), (0, 0)))
        array = array.reshape(-1, count, group, depth, rows)
        return jnp.transpose(array, (1, 0, 2, 3, 4))

    def from_heads(array):
        array = array.reshape(-1, padded, depth, rows)
        return array[:, :HEADS].reshape(-1, rows)

    mixed_heads = scattered(to_heads(mixed))
    out_heads, lse = attention_forward(ranks, mixed_heads)
    attended = from_heads(returned(out_heads, 0))
    attended_own = part_of(attended, core, half_width)
    attended_other = part_of(attended, 1 - core, half_width)
    branch = contract(attended_own, w_proj, 0, 0) + contract(attended_other, other_proj, 0, 0)
    middle = inputs + branch + wide(proj_bias)

    normed_two, norm_two_pull = jax.vjp(layer_norm, middle, wide(ln2_gain), wide(ln2_bias))
    normed_two_low = normed_two.astype(low_type)
    rows_two = jnp.concatenate([normed_two_low, swapped(normed_two_low)], axis=0)
    index = lax.axis_index("dp")
    low_high, top_high = lax.rem(index, 2), lax.div(index, 1 << (bits - 1))
    half_units = w_down.shape[0] // 2
    rows_two_near = lax.ppermute(rows_two, "dp", dp_hops(bits - 1))
    pre_act = contract(w_up, rows_two, 0, 1) + wide(up_bias)[:, None]
    activated, gelu_pull = jax.vjp(gelu_tanh, pre_act)
    act_low = row_major(activated.astype(low_type))
    act_near = lax.ppermute(part_of(act_low, 1 - low_high, half_units), "dp", dp_hops(0))
    grad_pre = row_major(gelu_pull(grad_act)[0].astype(low_type))
    grad_pre_near = lax.ppermute(part_of(grad_pre, 1 - top_high, half_units), "dp", dp_hops(bits - 1))
    grad_up_bias = jnp.sum(wide(grad_pre), axis=1)

    back_terms = contract(grad_pre, w_up, 0, 1)
    grad_norm_two = back_terms[:rows] + wide(swapped(back_terms[rows:].astype(low_type)))
    grad_out = wide(grad_low)
    grad_down_bias = jnp.sum(grad_out, axis=0)
    grad_mid_norm, grad_ln2_gain, grad_ln2_bias = norm_two_pull(grad_norm_two)
    grad_mid = grad_out + grad_mid_norm
    grad_branch = grad_mid.astype(low_type)
    grad_proj_bias = jnp.sum(wide(grad_branch), axis=0)
    grad_attended = in_order(
        contract(w_proj, grad_branch, 1, 1).astype(low_type),
        contract(other_proj, grad_branch, 1, 1).astype(low_type),
        core == 1,
        0,
    )
    grad_heads = scattered(to_heads(grad_attended))[:, 0]

    grad_heads, act_later, grad_pre_later = tied(grad_heads, act_low, grad_pre)
    grad_w_down = contract(part_of(act_later, low_high, half_units), grad_rows, 1, 0) + contract(
        act_near, grad_rows_near, 1, 0
    )
    grad_w_up = contract(rows_two, part_of(grad_pre_later, top_high, half_units), 0, 1) + contract(
        rows_two_near, grad_pre_near, 0, 1
    )
    grad_w_down = row_major(grad_w_down.astype(low_type))
    grad_w_up = row_major(grad_w_up.astype(low_type))
    grad_heads, grad_w_down, grad_w_up = tied(grad_heads, grad_w_down, grad_w_up)
    down_share = reduced(grad_w_down, upward[1:])
    up_share = reduced(grad_w_up, downward[1:])

    grad_mixed_heads = attention_backward(ranks, mixed_heads, out_heads, grad_heads, lse)
    (grad_mixed_heads, act_late, attended_late, branch_late, down_share, up_share) = tied(
        grad_mixed_heads, act_low, attended_other, grad_branch, down_share, up_share
    )
    down_share, up_share = lax.psum((down_share, up_share), "ctx")
    grad_mixed = from_heads(returned(grad_mixed_heads, 1))
    query_rows = lax.broadcasted_iota(jnp.int32, (3 * width, 1), 0) < width
    grad_mixed = jnp.where(query_rows, grad_mixed * low_type(scale), grad_mixed)
    grad_mixed_sums = jnp.sum(wide(grad_mixed), axis=1)

    down_terms = contract(act_late, w_down, 0, 0)
    mlp_sum = down_terms[:rows] + wide(swapped(down_terms[rows:].astype(low_type)))
    output = by_rows((middle + mlp_sum + wide(down_bias)).astype(low_type))

    attended_both = jnp.concatenate([attended_own, swapped(attended_late)], axis=1)
    branch_both = jnp.concatenate([branch_late, swapped(branch_late)], axis=0)
    grad_w_proj = contract(attended_both, branch_both, 1, 0)
    proj_share = reduced(row_major(grad_w_proj.astype(low_type)), downward)

    small_early = own_half(
        jnp.stack(
            [
                grad_mixed_sums[:width],
                grad_mixed_sums[2 * width :],
                grad_proj_bias,
                grad_ln2_gain,
                grad_ln2_bias,
                grad_down_bias,
            ]
        )
    )
    wide_rows = -(-grad_up_bias.shape[0] // half_width)
    up_bias_rows = jnp.pad(grad_up_bias, (0, wide_rows * half_width - grad_up_bias.shape[0]))
    small_early = jnp.concatenate([small_early, up_bias_rows.reshape(wide_rows, half_width)])

    normed_both = jnp.concatenate([normed_own, swapped(normed_other)], axis=0)
    grad_mixed_both = jnp.concatenate([grad_mixed, swapped(grad_mixed)], axis=1)
    grad_w_qkv = contract(normed_both, grad_mixed_both, 0, 1)
    grad_w_qkv = row_major(grad_w_qkv.astype(low_type))
    first_share = reduced(grad_w_qkv[:, : 2 * width], upward)
    second_share = reduced(grad_w_qkv[:, 2 * width :], downward)

    (down_share, up_share, first_share, second_share, proj_share, small_later) = tied(
        down_share, up_share, first_share, second_share, proj_share, small_early
    )
    down_total = wide(joined(*halves_of_all(down_share, (0,) * bits), bits))
    up_total = wide(joined(*halves_of_all(up_share, (0,) * (bits - 1) + (1,)), bits - 1))
    first_share, second_share, proj_share = lax.psum((first_share, second_share, proj_share), "ctx")
    qkv_total = jnp.concatenate(
        [wide(spread(first_share, upward)), wide(spread(second_share, downward))], axis=1
    )
    proj_total = wide(spread(proj_share, downward))

    grad_norm_one = in_order(
        contract(grad_mixed, w_qkv, 0, 1), contract(grad_mixed, other_qkv, 0, 1), core == 1, 1
    )
    grad_in_norm, grad_ln1_gain, grad_ln1_bias = norm_one_pull(grad_norm_one)
    grad_hidden = by_rows((grad_mid + grad_in_norm).astype(low_type))

    small_rows = jnp.stack([grad_ln1_gain, grad_ln1_bias])
    small_own = own_half(small_rows)
    small_total = small_total_over_group(jnp.concatenate([small_own, small_later]))
    up_bias_total = small_total[8:].reshape(-1)[: grad_up_bias.shape[0]]
    return (
        output,
        grad_hidden,
        small_total[0],
        small_total[1],
        qkv_total,
        small_total[2],
        small_total[3],
        proj_total,
        small_total[4],
        small_total[5],
        small_total[6],
        up_total,
        up_bias_total,
        down_total,
        small_total[7],
    )


def solution(mesh):
    placed = (
        P("dp", ("ctx", "wt"), None),
        P(),
        P(),
        P(),
        P("wt", None),
        P(),
        P(),
        P("wt", None),
        P(),
        P(),
        P(),
        P(None, "wt"),
        P("wt"),
        P("wt", None),
        P(),
        P("dp", ("ctx", "wt"), None),
    )
    return jax.shard_map(
        local,
        mesh=mesh,
        in_specs=placed,
        out_specs=(
            P("dp", ("ctx", "wt"), None),
            P("dp", ("ctx", "wt"), None),
            P("wt"),
            P("wt"),
            P("wt", None),
            P("wt"),
            P("wt"),
            P("wt", None),
            P("wt"),
            P("wt"),
            P("wt"),
            P(None, "wt"),
            P("wt"),
            P("wt", None),
            P("wt"),
        ),
        check_vma=False,
    )
```

```python
import math

import jax
import jax.numpy as jnp
from jax import lax
from jax.experimental import pallas as pl
from jax.experimental.layout import Layout, with_layout_constraint
from jax.experimental.pallas import tpu as pltpu
from jax.sharding import PartitionSpec as P

HEADS = 17

epsilon = 1e-05
masked_value = -1e30
low_type = jnp.bfloat16
full_type = jnp.float32


def wide(array):
    return array.astype(full_type)


def layer_norm(values, gain, offset):
    average = jnp.mean(values, axis=-1, keepdims=True)
    shifted = values - average
    variance = jnp.mean(shifted * shifted, axis=-1, keepdims=True)
    return shifted * lax.rsqrt(variance + epsilon) * gain + offset


def gelu_tanh(values):
    return jax.nn.gelu(values, approximate=True)


def contract(first, second, first_dim, second_dim):
    return lax.dot_general(
        first, second, (((first_dim,), (second_dim,)), ((), ())), preferred_element_type=full_type
    )


def repeat(start, stop, body, carry):
    if isinstance(start, int) and isinstance(stop, int) and stop - start <= 4:
        for index in range(start, stop):
            carry = body(index, carry)
        return carry
    return lax.fori_loop(start, stop, body, carry)


def pair_of(ref, index):
    return jnp.concatenate([ref[2 * index], ref[2 * index + 1]], axis=-1)


def put_pair(ref, index, tile):
    half = tile.shape[-1] // 2
    ref[2 * index] = tile[:, :half].astype(ref.dtype)
    ref[2 * index + 1] = tile[:, half:].astype(ref.dtype)


def causal(scores):
    key_at = lax.broadcasted_iota(jnp.int32, scores.shape, 0)
    query_at = lax.broadcasted_iota(jnp.int32, scores.shape, 1)
    return jnp.where(key_at <= query_at, scores, masked_value)


def forward_kernel(ranks, mixed_ref, out_ref, lse_ref, queries, keys, values, outs):
    count = mixed_ref.shape[0]
    block = mixed_ref.shape[-1] // 2
    for piece in range(count):
        for half in range(2):
            rank = ranks[2 * piece + half]
            span = slice(half * block, (half + 1) * block)
            queries[rank] = mixed_ref[piece, 0, 0, :, span]
            keys[rank] = mixed_ref[piece, 1, 0, :, span]
            values[rank] = mixed_ref[piece, 2, 0, :, span]

    def query_tile(at, unused):
        query = pair_of(queries, at)

        def scores_at(key_at, diagonal=False):
            scores = contract(pair_of(keys, key_at), query, 0, 0)
            return causal(scores) if diagonal else scores

        def key_tile(key_at, carry, diagonal=False):
            highest, total, accum = carry
            scores = scores_at(key_at, diagonal)
            new_highest = jnp.maximum(highest, jnp.max(scores, axis=0, keepdims=True))
            probs = jnp.exp(scores - new_highest)
            shrink = jnp.exp(highest - new_highest)
            total = total * shrink + jnp.sum(probs, axis=0, keepdims=True)
            accum = accum * shrink + contract(
                pair_of(values, key_at), probs.astype(low_type), 1, 0
            )
            return new_highest, total, accum

        if isinstance(at, int):
            tiles = [scores_at(key_at, key_at == at) for key_at in range(at + 1)]
            highest = jnp.max(tiles[0], axis=0, keepdims=True)
            for tile in tiles[1:]:
                highest = jnp.maximum(highest, jnp.max(tile, axis=0, keepdims=True))
            total = jnp.zeros((1, 2 * block), full_type)
            accum = jnp.zeros(query.shape, full_type)
            for key_at, tile in enumerate(tiles):
                probs = jnp.exp(tile - highest)
                total = total + jnp.sum(probs, axis=0, keepdims=True)
                accum = accum + contract(pair_of(values, key_at), probs.astype(low_type), 1, 0)
        else:
            start = (
                jnp.full((1, 2 * block), masked_value, full_type),
                jnp.zeros((1, 2 * block), full_type),
                jnp.zeros(query.shape, full_type),
            )
            carry = lax.fori_loop(0, at, key_tile, start)
            highest, total, accum = key_tile(at, carry, True)
        put_pair(outs, at, accum / total)
        lse_ref[0, pl.ds(at, 1), :] = highest + jnp.log(total)
        return unused

    repeat(0, count, query_tile, 0)
    for piece in range(count):
        for half in range(2):
            rank = ranks[2 * piece + half]
            out_ref[piece, 0, :, half * block : (half + 1) * block] = outs[rank]


def backward_kernel(
    ranks,
    mixed_ref,
    out_ref,
    grad_ref,
    lse_ref,
    result_ref,
    queries,
    keys,
    values,
    outs,
    grads,
    query_grads,
    key_grads,
    value_grads,
    deltas,
):
    count = mixed_ref.shape[0]
    block = mixed_ref.shape[-1] // 2
    for piece in range(count):
        for half in range(2):
            rank = ranks[2 * piece + half]
            span = slice(half * block, (half + 1) * block)
            queries[rank] = mixed_ref[piece, 0, 0, :, span]
            keys[rank] = mixed_ref[piece, 1, 0, :, span]
            values[rank] = mixed_ref[piece, 2, 0, :, span]
            outs[rank] = out_ref[piece, 0, :, span]
            grads[rank] = grad_ref[piece, 0, :, span]

    def delta_tile(at, unused):
        terms = pair_of(outs, at).astype(full_type) * pair_of(grads, at).astype(full_type)
        deltas[pl.ds(at, 1), :] = jnp.sum(terms, axis=0, keepdims=True)
        zeros = jnp.zeros(query_grads.shape[1:], full_type)
        query_grads[2 * at] = zeros
        query_grads[2 * at + 1] = zeros
        return unused

    repeat(0, count, delta_tile, 0)

    def key_tile(key_at, unused):
        key = pair_of(keys, key_at)
        value = pair_of(values, key_at)

        def query_tile(at, carry, diagonal=False):
            key_grad, value_grad = carry
            query = pair_of(queries, at)
            grad = pair_of(grads, at)
            scores = contract(key, query, 0, 0)
            if diagonal:
                scores = causal(scores)
            probs = jnp.exp(scores - lse_ref[0, pl.ds(at, 1), :])
            grad_probs = contract(value, grad, 0, 0)
            grad_scores = (probs * (grad_probs - deltas[pl.ds(at, 1), :])).astype(low_type)
            value_grad = value_grad + contract(grad, probs.astype(low_type), 1, 1)
            key_grad = key_grad + contract(query, grad_scores, 1, 1)
            query_grad = contract(key, grad_scores, 1, 0)
            query_grads[2 * at] += query_grad[:, :block]
            query_grads[2 * at + 1] += query_grad[:, block:]
            return key_grad, value_grad

        start = (jnp.zeros(key.shape, full_type), jnp.zeros(key.shape, full_type))
        carry = query_tile(key_at, start, True)
        key_grad, value_grad = repeat(key_at + 1, count, query_tile, carry)
        put_pair(key_grads, key_at, key_grad)
        put_pair(value_grads, key_at, value_grad)
        return unused

    repeat(0, count, key_tile, 0)
    for piece in range(count):
        for half in range(2):
            rank = ranks[2 * piece + half]
            span = slice(half * block, (half + 1) * block)
            result_ref[piece, 0, 0, :, span] = query_grads[rank].astype(low_type)
            result_ref[piece, 1, 0, :, span] = key_grads[rank]
            result_ref[piece, 2, 0, :, span] = value_grads[rank]


def attention_forward(ranks, mixed):
    count, _, heads, depth, rows = mixed.shape
    blocks = (2 * count, depth, rows // 2)
    return pl.pallas_call(
        forward_kernel,
        out_shape=(
            jax.ShapeDtypeStruct((count, heads, depth, rows), low_type),
            jax.ShapeDtypeStruct((heads, count, rows), full_type),
        ),
        grid_spec=pltpu.PrefetchScalarGridSpec(
            num_scalar_prefetch=1,
            grid=(heads,),
            in_specs=[
                pl.BlockSpec((count, 3, 1, depth, rows), lambda head, _: (0, 0, head, 0, 0))
            ],
            out_specs=(
                pl.BlockSpec((count, 1, depth, rows), lambda head, _: (0, head, 0, 0)),
                pl.BlockSpec((1, count, rows), lambda head, _: (head, 0, 0)),
            ),
            scratch_shapes=[pltpu.VMEM(blocks, low_type) for _ in range(4)],
        ),
        compiler_params=pltpu.CompilerParams(vmem_limit_bytes=40 * 2**20),
        cost_estimate=pl.CostEstimate(
            flops=2 * heads * count * (count + 1) * rows * rows * depth,
            bytes_accessed=8 * heads * count * depth * rows,
            transcendentals=heads * count * (count + 1) * rows * rows // 2,
        ),
    )(ranks, mixed)


def attention_backward(ranks, mixed, outs, grads, lse, part):
    count, _, _, depth, rows = mixed.shape
    start, stop = part
    blocks = (2 * count, depth, rows // 2)
    three_block = (count, 3, 1, depth, rows)
    three = pl.BlockSpec(three_block, lambda head, _: (0, 0, head + start, 0, 0))
    one = pl.BlockSpec((count, 1, depth, rows), lambda head, _: (0, head + start, 0, 0))
    return pl.pallas_call(
        backward_kernel,
        out_shape=jax.ShapeDtypeStruct((count, 3, stop - start, depth, rows), low_type),
        grid_spec=pltpu.PrefetchScalarGridSpec(
            num_scalar_prefetch=1,
            grid=(stop - start,),
            in_specs=[
                three,
                one,
                one,
                pl.BlockSpec((1, count, rows), lambda head, _: (head + start, 0, 0)),
            ],
            out_specs=pl.BlockSpec(three_block, lambda head, _: (0, 0, head, 0, 0)),
            scratch_shapes=[pltpu.VMEM(blocks, low_type) for _ in range(5)]
            + [pltpu.VMEM(blocks, full_type)]
            + [pltpu.VMEM(blocks, low_type) for _ in range(2)]
            + [pltpu.VMEM((count, rows), full_type)],
        ),
        compiler_params=pltpu.CompilerParams(vmem_limit_bytes=40 * 2**20),
        cost_estimate=pl.CostEstimate(flops=0, bytes_accessed=0, transcendentals=0),
    )(ranks, mixed, outs, grads, lse)


def swapped(array):
    return lax.ppermute(array, "wt", [(0, 1), (1, 0)])


def part_of(array, index, size, axis=0):
    return lax.dynamic_slice_in_dim(array, index * size, size, axis)


def in_order(first, second, flip, axis):
    return jnp.where(
        flip, jnp.concatenate([second, first], axis), jnp.concatenate([first, second], axis)
    )


def scattered(send):
    count = lax.axis_size("ctx")
    place = lax.axis_index("ctx")
    pieces = []
    for shift in range(count):
        piece = lax.dynamic_index_in_dim(send, lax.rem(place + shift, count), 0, False)
        if shift:
            hops = [(one, (one + shift) % count) for one in range(count)]
            piece = lax.ppermute(piece, "ctx", hops)
        pieces.append(piece)
    return jnp.stack(pieces)


def sent_back(pieces):
    count = lax.axis_size("ctx")
    back = [pieces[0]]
    for shift in range(1, count):
        hops = [(one, (one - shift) % count) for one in range(count)]
        back.append(lax.ppermute(pieces[shift], "ctx", hops))
    return back


def assembled(backs, parts):
    count = len(backs[0])
    lead, (depth, rows) = backs[0][0].shape[:-3], backs[0][0].shape[-2:]
    result = jnp.zeros((*lead, count, parts[-1][1], depth, rows), low_type)
    for back, (start, _) in zip(backs, parts):
        for shift, piece in enumerate(back):
            source = lax.rem(lax.axis_index("ctx") + shift, count)
            at = (0,) * len(lead) + (source, start, 0, 0)
            result = lax.dynamic_update_slice(result, jnp.expand_dims(piece, len(lead)), at)
    return result


def pair_hops(axis, bit):
    return [(one, one ^ (1 << bit)) for one in range(lax.axis_size(axis))]


def bit_of(axis, bit):
    return lax.rem(lax.div(lax.axis_index(axis), 1 << bit), 2)


def reduced(array, axis, order):
    for bit in order:
        half = array.shape[0] // 2
        high = bit_of(axis, bit)
        kept = part_of(array, high, half)
        arrived = lax.ppermute(part_of(array, 1 - high, half), axis, pair_hops(axis, bit))
        array = (wide(kept) + wide(arrived)).astype(low_type)
    return array


def spread(array, axis, order, dim=0):
    for bit in order:
        arrived = lax.ppermute(array, axis, pair_hops(axis, bit))
        array = in_order(array, arrived, bit_of(axis, bit) == 1, dim)
    return array


def spread_both(parts, dims, step):
    order = range(len(dims))
    return tuple(
        spread(part, "dp", (bits[step],), dims[bits[step]])
        for part, bits in zip(parts, (order, order[::-1]))
    )


def in_two(array):
    half = array.shape[0] // 2
    return array[:half], array[half:]


def joined(parts, bits):
    forth, back = parts
    forth = forth.reshape((2,) * bits + (-1, forth.shape[1]))
    forth = jnp.transpose(forth, (*reversed(range(bits)), bits, bits + 1))
    return jnp.stack([forth, back.reshape(forth.shape)], axis=bits).reshape(-1, forth.shape[-1])


def row_major(array):
    return with_layout_constraint(array, Layout(major_to_minor=(0, 1)))


def tied(*arrays):
    return lax.optimization_barrier(arrays)


def summed(array, axis, order):
    for bit in order:
        array = array + lax.ppermute(array, axis, pair_hops(axis, bit))
    return array


def local(
    hidden,
    block_order,
    ln1_gain,
    ln1_bias,
    w_qkv,
    q_bias,
    v_bias,
    w_proj,
    proj_bias,
    ln2_gain,
    ln2_bias,
    w_up,
    up_bias,
    w_down,
    down_bias,
    cotangent,
):
    seqs, seq_dev, width = hidden.shape
    depth = width // HEADS
    scale = 1.0 / math.sqrt(depth)
    count = lax.axis_size("ctx")
    place = lax.axis_index("ctx")
    core = lax.axis_index("wt")
    half_width = width // 2
    rows = 2 * seq_dev
    group = -(-HEADS // count)
    padded = group * count
    bits = int(math.log2(lax.axis_size("dp")))
    upward = tuple(range(bits))
    downward = tuple(reversed(upward))

    def by_sequence(array):
        mine = lax.dynamic_index_in_dim(array, core, 0, False)
        theirs = lax.dynamic_index_in_dim(array, 1 - core, 0, False)
        return jnp.concatenate([mine, swapped(theirs)], axis=0)

    def by_rows(array):
        mine = array[:seq_dev]
        arrived = swapped(array[seq_dev:])
        return in_order(mine[None], arrived[None], core == 1, 0)

    sources = lax.rem(place - jnp.arange(count, dtype=jnp.int32) + count, count)
    slots = jnp.stack([2 * sources + core, 2 * sources + 1 - core], axis=1).reshape(-1)
    ranks = block_order[slots]

    rows_low = by_sequence(hidden)
    other_qkv = swapped(w_qkv)
    other_proj = swapped(w_proj)
    grad_low = by_sequence(cotangent)
    grad_rows = jnp.concatenate([grad_low, swapped(grad_low)], axis=0)
    grad_rows_near = lax.ppermute(grad_rows, "dp", pair_hops("dp", 0))
    grad_act = contract(w_down, grad_rows, 1, 1)

    inputs = wide(rows_low)
    normed, norm_one_pull = jax.vjp(layer_norm, inputs, wide(ln1_gain), wide(ln1_bias))
    normed_low = normed.astype(low_type)
    normed_own = part_of(normed_low, core, half_width, 1)
    normed_other = part_of(normed_low, 1 - core, half_width, 1)
    mixed = contract(w_qkv, normed_own, 0, 1) + contract(other_qkv, normed_other, 0, 1)
    offsets = jnp.concatenate([wide(q_bias), jnp.zeros((width,), full_type), wide(v_bias)])
    scales = jnp.concatenate([jnp.full((width,), scale, full_type), jnp.ones((2 * width,), full_type)])
    mixed = ((mixed + offsets[:, None]) * scales[:, None]).astype(low_type)

    def own_half(array):
        return part_of(array, core, half_width, 1) + swapped(
            part_of(array, 1 - core, half_width, 1)
        )

    def to_heads(array):
        array = array.reshape(-1, HEADS, depth, rows)
        array = jnp.pad(array, ((0, 0), (0, padded - HEADS), (0, 0), (0, 0)))
        array = array.reshape(-1, count, group, depth, rows)
        return jnp.transpose(array, (1, 0, 2, 3, 4))

    def from_heads(array):
        array = array.reshape(-1, padded, depth, rows)
        return array[:, :HEADS].reshape(-1, rows)

    normed_near = swapped(normed_other)
    mixed_heads, grad_act, grad_rows_near, normed_near = tied(
        scattered(to_heads(mixed)), grad_act, grad_rows_near, normed_near
    )
    out_heads, lse = attention_forward(ranks, mixed_heads)
    attended = from_heads(assembled([sent_back(out_heads)], ((0, group),)))
    attended_own = part_of(attended, core, half_width)
    attended_other = part_of(attended, 1 - core, half_width)
    branch = contract(attended_own, w_proj, 0, 0) + contract(attended_other, other_proj, 0, 0)
    middle = inputs + branch + wide(proj_bias)

    normed_two, norm_two_pull = jax.vjp(layer_norm, middle, wide(ln2_gain), wide(ln2_bias))
    normed_two_low, attended_near = tied(normed_two.astype(low_type), swapped(attended_other))
    rows_two = jnp.concatenate([normed_two_low, swapped(normed_two_low)], axis=0)
    low_high, top_high = bit_of("dp", 0), bit_of("dp", bits - 1)
    half_units = w_down.shape[0] // 2
    pre_act = contract(w_up, rows_two, 0, 1) + wide(up_bias)[:, None]
    activated, gelu_pull = jax.vjp(gelu_tanh, pre_act)
    act_low = row_major(activated.astype(low_type))
    act_near = lax.ppermute(part_of(act_low, 1 - low_high, half_units), "dp", pair_hops("dp", 0))
    grad_pre = row_major(gelu_pull(grad_act)[0].astype(low_type))
    up_send = jnp.concatenate([rows_two.T, part_of(grad_pre, 1 - top_high, half_units)])
    up_send, grad_pre = tied(up_send, grad_pre)
    up_near = lax.ppermute(up_send, "dp", pair_hops("dp", bits - 1))
    grad_up_bias = jnp.sum(wide(grad_pre), axis=1)

    back_terms = contract(grad_pre, w_up, 0, 1)
    grad_norm_two = back_terms[:rows] + wide(swapped(back_terms[rows:].astype(low_type)))
    grad_out = wide(grad_low)
    grad_down_bias = jnp.sum(grad_out, axis=0)
    grad_mid_norm, grad_ln2_gain, grad_ln2_bias = norm_two_pull(grad_norm_two)
    grad_mid = grad_out + grad_mid_norm
    grad_branch = grad_mid.astype(low_type)
    grad_proj_bias = jnp.sum(wide(grad_branch), axis=0)
    grad_attended = in_order(
        contract(w_proj, grad_branch, 1, 1).astype(low_type),
        contract(other_proj, grad_branch, 1, 1).astype(low_type),
        core == 1,
        0,
    )
    grad_heads = scattered(to_heads(grad_attended))[:, 0]
    branch_near = swapped(grad_branch)

    grad_w_down = contract(grad_rows, part_of(act_low, low_high, half_units), 0, 1) + contract(
        grad_rows_near, act_near, 0, 1
    )
    grad_heads, grad_w_down, branch_near = tied(
        grad_heads, row_major(grad_w_down.astype(low_type)), branch_near
    )
    down_share = reduced(grad_w_down, "dp", upward[1:])

    cut = (group + 1) // 2
    parts = ((0, cut), (cut, group)) if cut < group else ((0, group),)
    grads_of = [
        attention_backward(ranks, mixed_heads, out_heads, grad_heads, lse, part) for part in parts
    ]
    grads_of[0], grad_pre_late = tied(grads_of[0], grad_pre)
    grad_w_up = contract(rows_two, part_of(grad_pre_late, top_high, half_units), 0, 1) + contract(
        up_near[:width], up_near[width:], 1, 1
    )
    grad_w_up = row_major(grad_w_up.astype(low_type))
    backs = [sent_back(grads_of[0])]
    for later in grads_of[1:]:
        backs[-1], later, grad_w_up, branch_late, down_share = tied(
            backs[-1], later, grad_w_up, grad_branch, down_share
        )
        backs.append(sent_back(later))
    turns = int(math.log2(count))
    down_share = reduced(down_share, "ctx", range(turns))
    up_share = reduced(grad_w_up, "dp", downward[1:])
    attended_both = jnp.concatenate([attended_own, attended_near], axis=1)
    branch_both = jnp.concatenate([grad_branch if cut == group else branch_late, branch_near])
    grad_w_proj = contract(attended_both, branch_both, 1, 0)
    grad_mixed, up_share, grad_w_proj, down_share = tied(
        from_heads(assembled(backs, parts)), up_share, grad_w_proj, down_share
    )
    query_rows = lax.broadcasted_iota(jnp.int32, (3 * width, 1), 0) < width
    grad_mixed = jnp.where(query_rows, grad_mixed * low_type(scale), grad_mixed)
    grad_mixed_sums = jnp.sum(wide(grad_mixed), axis=1)

    small_early = own_half(
        jnp.stack(
            [
                grad_mixed_sums[:width],
                grad_mixed_sums[2 * width :],
                grad_proj_bias,
                grad_ln2_gain,
                grad_ln2_bias,
                grad_down_bias,
            ]
        )
    )
    wide_rows = -(-grad_up_bias.shape[0] // half_width)
    up_bias_rows = jnp.pad(grad_up_bias, (0, wide_rows * half_width - grad_up_bias.shape[0]))
    small_early = jnp.concatenate([small_early, up_bias_rows.reshape(wide_rows, half_width)])

    normed_both = jnp.concatenate([normed_own, normed_near], axis=0)
    grad_mixed_both = jnp.concatenate([grad_mixed, swapped(grad_mixed)], axis=1)
    grad_w_qkv = contract(normed_both, grad_mixed_both, 0, 1)

    first = row_major(grad_w_qkv[:, : 2 * width].astype(low_type))
    second = row_major(
        jnp.concatenate([grad_w_qkv[:, 2 * width :], grad_w_proj], axis=1).astype(low_type)
    )
    first, second, up_share, down_share = tied(first, second, up_share, down_share)

    first, second = reduced(first, "dp", upward[:1]), reduced(second, "dp", downward[:1])
    up_share = reduced(up_share, "ctx", range(1))
    down_share = spread(down_share, "ctx", range(1, turns)[::-1])
    first, second, up_share, down_share, act_late, small_late = tied(
        first, second, up_share, down_share, act_low, small_early
    )

    down_terms = contract(act_late, w_down, 0, 0)
    mlp_sum = down_terms[:rows] + wide(swapped(down_terms[rows:].astype(low_type)))
    output = by_rows((middle + mlp_sum + wide(down_bias)).astype(low_type))

    down_dims = (1,) + (0,) * (bits - 1)
    up_dims = (0,) * (bits - 1) + (1,)
    first, second = reduced(first, "dp", upward[1:]), reduced(second, "dp", downward[1:])
    up_share = reduced(up_share, "ctx", range(1, turns))
    down_share = spread(down_share, "ctx", range(1))
    first, second, up_share, down_share, output, grad_mixed = tied(
        first, second, up_share, down_share, output, grad_mixed
    )

    last = jnp.concatenate([first, second])
    sliced = last.shape[0] % count == 0
    down_parts = spread_both(in_two(down_share), down_dims, 0)
    up_share = spread(up_share, "ctx", range(1, turns)[::-1])
    last = reduced(last, "ctx", range(1)) if sliced else lax.psum(last, "ctx")
    grad_norm_one = in_order(
        contract(grad_mixed, w_qkv, 0, 1), contract(grad_mixed, other_qkv, 0, 1), core == 1, 1
    )
    down_parts, up_share, last, grad_norm_one, small_late = tied(
        down_parts, up_share, last, grad_norm_one, small_late
    )

    down_parts = spread_both(down_parts, down_dims, 1)
    up_share = spread(up_share, "ctx", range(1))
    last = reduced(last, "ctx", range(1, turns)) if sliced else last
    grad_in_norm, grad_ln1_gain, grad_ln1_bias = norm_one_pull(grad_norm_one)
    grad_hidden = by_rows((grad_mid + grad_in_norm).astype(low_type))
    small = jnp.concatenate([own_half(jnp.stack([grad_ln1_gain, grad_ln1_bias])), small_late])
    down_parts, up_share, last, small, grad_hidden = tied(
        down_parts, up_share, last, small, grad_hidden
    )

    down_total = wide(joined(down_parts, bits - 1)).T
    up_parts = spread_both(in_two(up_share), up_dims, 0)
    last = spread(last, "ctx", range(1, turns)[::-1]) if sliced else last
    small = summed(small, "dp", upward[:1])
    up_parts, last, small = tied(up_parts, last, small)

    up_parts = spread_both(up_parts, up_dims, 1)
    last = spread(last, "ctx", range(1)) if sliced else last
    small = summed(small, "dp", upward[1:])
    up_parts, last, small, down_total = tied(up_parts, last, small, down_total)

    up_total = wide(joined(up_parts, bits - 1))
    first, second = in_two(last)
    first, second = spread(first, "dp", downward[:1]), spread(second, "dp", upward[:1])
    small = summed(small, "ctx", range(1))
    first, second, small, up_total = tied(first, second, small, up_total)

    small_total = summed(small, "ctx", range(1, turns))
    first, second = spread(first, "dp", downward[1:]), spread(second, "dp", upward[1:])
    qkv_total = jnp.concatenate([wide(first), wide(second[:, :width])], axis=1)
    proj_total = wide(second[:, width:])
    up_bias_total = small_total[8:].reshape(-1)[: grad_up_bias.shape[0]]
    return (
        output,
        grad_hidden,
        small_total[0],
        small_total[1],
        qkv_total,
        small_total[2],
        small_total[3],
        proj_total,
        small_total[4],
        small_total[5],
        small_total[6],
        up_total,
        up_bias_total,
        down_total,
        small_total[7],
    )


def solution(mesh):
    placed = (
        P("dp", ("ctx", "wt"), None),
        P(),
        P(),
        P(),
        P("wt", None),
        P(),
        P(),
        P("wt", None),
        P(),
        P(),
        P(),
        P(None, "wt"),
        P("wt"),
        P("wt", None),
        P(),
        P("dp", ("ctx", "wt"), None),
    )
    return jax.shard_map(
        local,
        mesh=mesh,
        in_specs=placed,
        out_specs=(
            P("dp", ("ctx", "wt"), None),
            P("dp", ("ctx", "wt"), None),
            P("wt"),
            P("wt"),
            P("wt", None),
            P("wt"),
            P("wt"),
            P("wt", None),
            P("wt"),
            P("wt"),
            P("wt"),
            P(None, "wt"),
            P("wt"),
            P("wt", None),
            P("wt"),
        ),
        check_vma=False,
    )
```

```python
import math

import jax
import jax.numpy as jnp
from jax import lax
from jax.experimental import pallas as pl
from jax.experimental.layout import Layout, with_layout_constraint
from jax.experimental.pallas import tpu as pltpu
from jax.sharding import PartitionSpec as P

HEADS = 17

epsilon = 1e-05
masked_value = -1e30
low_type = jnp.bfloat16
full_type = jnp.float32


def wide(array):
    return array.astype(full_type)


def layer_norm(values, gain, offset):
    average = jnp.mean(values, axis=-1, keepdims=True)
    shifted = values - average
    variance = jnp.mean(shifted * shifted, axis=-1, keepdims=True)
    return shifted * lax.rsqrt(variance + epsilon) * gain + offset


def gelu_tanh(values):
    return jax.nn.gelu(values, approximate=True)


def contract(first, second, first_dim, second_dim):
    return lax.dot_general(
        first, second, (((first_dim,), (second_dim,)), ((), ())), preferred_element_type=full_type
    )


def repeat(start, stop, body, carry):
    if isinstance(start, int) and isinstance(stop, int) and stop - start <= 4:
        for index in range(start, stop):
            carry = body(index, carry)
        return carry
    return lax.fori_loop(start, stop, body, carry)


def pair_of(ref, index):
    return jnp.concatenate([ref[2 * index], ref[2 * index + 1]], axis=-1)


def put_pair(ref, index, tile):
    half = tile.shape[-1] // 2
    ref[2 * index] = tile[:, :half].astype(ref.dtype)
    ref[2 * index + 1] = tile[:, half:].astype(ref.dtype)


def causal(scores):
    key_at = lax.broadcasted_iota(jnp.int32, scores.shape, 0)
    query_at = lax.broadcasted_iota(jnp.int32, scores.shape, 1)
    return jnp.where(key_at <= query_at, scores, masked_value)


def forward_kernel(ranks, mixed_ref, out_ref, lse_ref, queries, keys, values, outs):
    count = mixed_ref.shape[0]
    block = mixed_ref.shape[-1] // 2
    for piece in range(count):
        for half in range(2):
            rank = ranks[2 * piece + half]
            span = slice(half * block, (half + 1) * block)
            queries[rank] = mixed_ref[piece, 0, 0, :, span]
            keys[rank] = mixed_ref[piece, 1, 0, :, span]
            values[rank] = mixed_ref[piece, 2, 0, :, span]

    def query_tile(at, unused):
        query = pair_of(queries, at)

        def scores_at(key_at, diagonal=False):
            scores = contract(pair_of(keys, key_at), query, 0, 0)
            return causal(scores) if diagonal else scores

        def key_tile(key_at, carry, diagonal=False):
            highest, total, accum = carry
            scores = scores_at(key_at, diagonal)
            new_highest = jnp.maximum(highest, jnp.max(scores, axis=0, keepdims=True))
            probs = jnp.exp(scores - new_highest)
            shrink = jnp.exp(highest - new_highest)
            total = total * shrink + jnp.sum(probs, axis=0, keepdims=True)
            accum = accum * shrink + contract(
                pair_of(values, key_at), probs.astype(low_type), 1, 0
            )
            return new_highest, total, accum

        if isinstance(at, int):
            tiles = [scores_at(key_at, key_at == at) for key_at in range(at + 1)]
            highest = jnp.max(tiles[0], axis=0, keepdims=True)
            for tile in tiles[1:]:
                highest = jnp.maximum(highest, jnp.max(tile, axis=0, keepdims=True))
            total = jnp.zeros((1, 2 * block), full_type)
            accum = jnp.zeros(query.shape, full_type)
            for key_at, tile in enumerate(tiles):
                probs = jnp.exp(tile - highest)
                total = total + jnp.sum(probs, axis=0, keepdims=True)
                accum = accum + contract(pair_of(values, key_at), probs.astype(low_type), 1, 0)
        else:
            start = (
                jnp.full((1, 2 * block), masked_value, full_type),
                jnp.zeros((1, 2 * block), full_type),
                jnp.zeros(query.shape, full_type),
            )
            carry = lax.fori_loop(0, at, key_tile, start)
            highest, total, accum = key_tile(at, carry, True)
        put_pair(outs, at, accum / total)
        lse_ref[0, pl.ds(at, 1), :] = highest + jnp.log(total)
        return unused

    repeat(0, count, query_tile, 0)
    for piece in range(count):
        for half in range(2):
            rank = ranks[2 * piece + half]
            out_ref[piece, 0, :, half * block : (half + 1) * block] = outs[rank]


def backward_kernel(
    ranks,
    mixed_ref,
    out_ref,
    grad_ref,
    lse_ref,
    result_ref,
    queries,
    keys,
    values,
    outs,
    grads,
    query_grads,
    key_grads,
    value_grads,
    deltas,
):
    count = mixed_ref.shape[0]
    block = mixed_ref.shape[-1] // 2
    for piece in range(count):
        for half in range(2):
            rank = ranks[2 * piece + half]
            span = slice(half * block, (half + 1) * block)
            queries[rank] = mixed_ref[piece, 0, 0, :, span]
            keys[rank] = mixed_ref[piece, 1, 0, :, span]
            values[rank] = mixed_ref[piece, 2, 0, :, span]
            outs[rank] = out_ref[piece, 0, :, span]
            grads[rank] = grad_ref[piece, 0, :, span]

    def delta_tile(at, unused):
        terms = pair_of(outs, at).astype(full_type) * pair_of(grads, at).astype(full_type)
        deltas[pl.ds(at, 1), :] = jnp.sum(terms, axis=0, keepdims=True)
        zeros = jnp.zeros(query_grads.shape[1:], full_type)
        query_grads[2 * at] = zeros
        query_grads[2 * at + 1] = zeros
        return unused

    repeat(0, count, delta_tile, 0)

    def key_tile(key_at, unused):
        key = pair_of(keys, key_at)
        value = pair_of(values, key_at)

        def query_tile(at, carry, diagonal=False):
            key_grad, value_grad = carry
            query = pair_of(queries, at)
            grad = pair_of(grads, at)
            scores = contract(key, query, 0, 0)
            if diagonal:
                scores = causal(scores)
            probs = jnp.exp(scores - lse_ref[0, pl.ds(at, 1), :])
            grad_probs = contract(value, grad, 0, 0)
            grad_scores = (probs * (grad_probs - deltas[pl.ds(at, 1), :])).astype(low_type)
            value_grad = value_grad + contract(grad, probs.astype(low_type), 1, 1)
            key_grad = key_grad + contract(query, grad_scores, 1, 1)
            query_grad = contract(key, grad_scores, 1, 0)
            query_grads[2 * at] += query_grad[:, :block]
            query_grads[2 * at + 1] += query_grad[:, block:]
            return key_grad, value_grad

        start = (jnp.zeros(key.shape, full_type), jnp.zeros(key.shape, full_type))
        carry = query_tile(key_at, start, True)
        key_grad, value_grad = repeat(key_at + 1, count, query_tile, carry)
        put_pair(key_grads, key_at, key_grad)
        put_pair(value_grads, key_at, value_grad)
        return unused

    repeat(0, count, key_tile, 0)
    for piece in range(count):
        for half in range(2):
            rank = ranks[2 * piece + half]
            span = slice(half * block, (half + 1) * block)
            result_ref[piece, 0, 0, :, span] = query_grads[rank].astype(low_type)
            result_ref[piece, 1, 0, :, span] = key_grads[rank]
            result_ref[piece, 2, 0, :, span] = value_grads[rank]


def attention_forward(ranks, mixed):
    count, _, heads, depth, rows = mixed.shape
    blocks = (2 * count, depth, rows // 2)
    return pl.pallas_call(
        forward_kernel,
        out_shape=(
            jax.ShapeDtypeStruct((count, heads, depth, rows), low_type),
            jax.ShapeDtypeStruct((heads, count, rows), full_type),
        ),
        grid_spec=pltpu.PrefetchScalarGridSpec(
            num_scalar_prefetch=1,
            grid=(heads,),
            in_specs=[
                pl.BlockSpec((count, 3, 1, depth, rows), lambda head, _: (0, 0, head, 0, 0))
            ],
            out_specs=(
                pl.BlockSpec((count, 1, depth, rows), lambda head, _: (0, head, 0, 0)),
                pl.BlockSpec((1, count, rows), lambda head, _: (head, 0, 0)),
            ),
            scratch_shapes=[pltpu.VMEM(blocks, low_type) for _ in range(4)],
        ),
        compiler_params=pltpu.CompilerParams(vmem_limit_bytes=40 * 2**20),
        cost_estimate=pl.CostEstimate(
            flops=2 * heads * count * (count + 1) * rows * rows * depth,
            bytes_accessed=8 * heads * count * depth * rows,
            transcendentals=heads * count * (count + 1) * rows * rows // 2,
        ),
    )(ranks, mixed)


def attention_backward(ranks, mixed, outs, grads, lse, part):
    count, _, _, depth, rows = mixed.shape
    start, stop = part
    blocks = (2 * count, depth, rows // 2)
    three_block = (count, 3, 1, depth, rows)
    three = pl.BlockSpec(three_block, lambda head, _: (0, 0, head + start, 0, 0))
    one = pl.BlockSpec((count, 1, depth, rows), lambda head, _: (0, head + start, 0, 0))
    return pl.pallas_call(
        backward_kernel,
        out_shape=jax.ShapeDtypeStruct((count, 3, stop - start, depth, rows), low_type),
        grid_spec=pltpu.PrefetchScalarGridSpec(
            num_scalar_prefetch=1,
            grid=(stop - start,),
            in_specs=[
                three,
                one,
                one,
                pl.BlockSpec((1, count, rows), lambda head, _: (head + start, 0, 0)),
            ],
            out_specs=pl.BlockSpec(three_block, lambda head, _: (0, 0, head, 0, 0)),
            scratch_shapes=[pltpu.VMEM(blocks, low_type) for _ in range(5)]
            + [pltpu.VMEM(blocks, full_type)]
            + [pltpu.VMEM(blocks, low_type) for _ in range(2)]
            + [pltpu.VMEM((count, rows), full_type)],
        ),
        compiler_params=pltpu.CompilerParams(vmem_limit_bytes=40 * 2**20),
        cost_estimate=pl.CostEstimate(flops=0, bytes_accessed=0, transcendentals=0),
    )(ranks, mixed, outs, grads, lse)


def swapped(array):
    return lax.ppermute(array, "wt", [(0, 1), (1, 0)])


def part_of(array, index, size, axis=0):
    return lax.dynamic_slice_in_dim(array, index * size, size, axis)


def in_order(first, second, flip, axis):
    return jnp.where(
        flip, jnp.concatenate([second, first], axis), jnp.concatenate([first, second], axis)
    )


def scattered(send):
    count = lax.axis_size("ctx")
    place = lax.axis_index("ctx")
    pieces = []
    for shift in range(count):
        piece = lax.dynamic_index_in_dim(send, lax.rem(place + shift, count), 0, False)
        if shift:
            hops = [(one, (one + shift) % count) for one in range(count)]
            piece = lax.ppermute(piece, "ctx", hops)
        pieces.append(piece)
    return jnp.stack(pieces)


def sent_back(pieces):
    count = lax.axis_size("ctx")
    back = [pieces[0]]
    for shift in range(1, count):
        hops = [(one, (one - shift) % count) for one in range(count)]
        back.append(lax.ppermute(pieces[shift], "ctx", hops))
    return back


def assembled(backs, parts):
    count = len(backs[0])
    lead, (depth, rows) = backs[0][0].shape[:-3], backs[0][0].shape[-2:]
    result = jnp.zeros((*lead, count, parts[-1][1], depth, rows), low_type)
    for back, (start, _) in zip(backs, parts):
        for shift, piece in enumerate(back):
            source = lax.rem(lax.axis_index("ctx") + shift, count)
            at = (0,) * len(lead) + (source, start, 0, 0)
            result = lax.dynamic_update_slice(result, jnp.expand_dims(piece, len(lead)), at)
    return result


def pair_hops(axis, bit):
    return [(one, one ^ (1 << bit)) for one in range(lax.axis_size(axis))]


def bit_of(axis, bit):
    return lax.rem(lax.div(lax.axis_index(axis), 1 << bit), 2)


def reduced(array, axis, order):
    for bit in order:
        half = array.shape[0] // 2
        high = bit_of(axis, bit)
        kept = part_of(array, high, half)
        arrived = lax.ppermute(part_of(array, 1 - high, half), axis, pair_hops(axis, bit))
        array = (wide(kept) + wide(arrived)).astype(low_type)
    return array


def spread(array, axis, order, dim=0):
    for bit in order:
        arrived = lax.ppermute(array, axis, pair_hops(axis, bit))
        array = in_order(array, arrived, bit_of(axis, bit) == 1, dim)
    return array


def spread_both(parts, dims, step):
    order = range(len(dims))
    return tuple(
        spread(part, "dp", (bits[step],), dims[bits[step]])
        for part, bits in zip(parts, (order, order[::-1]))
    )


def in_two(array):
    half = array.shape[0] // 2
    return array[:half], array[half:]


def joined(parts, bits):
    forth, back = parts
    forth = forth.reshape((2,) * bits + (-1, forth.shape[1]))
    forth = jnp.transpose(forth, (*reversed(range(bits)), bits, bits + 1))
    return jnp.stack([forth, back.reshape(forth.shape)], axis=bits).reshape(-1, forth.shape[-1])


def row_major(array):
    return with_layout_constraint(array, Layout(major_to_minor=(0, 1)))


def tied(*arrays):
    return lax.optimization_barrier(arrays)


def summed(array, axis, order):
    for bit in order:
        array = array + lax.ppermute(array, axis, pair_hops(axis, bit))
    return array


def local(
    hidden,
    block_order,
    ln1_gain,
    ln1_bias,
    w_qkv,
    q_bias,
    v_bias,
    w_proj,
    proj_bias,
    ln2_gain,
    ln2_bias,
    w_up,
    up_bias,
    w_down,
    down_bias,
    cotangent,
):
    seqs, seq_dev, width = hidden.shape
    depth = width // HEADS
    scale = 1.0 / math.sqrt(depth)
    count = lax.axis_size("ctx")
    place = lax.axis_index("ctx")
    core = lax.axis_index("wt")
    half_width = width // 2
    rows = 2 * seq_dev
    group = -(-HEADS // count)
    padded = group * count
    bits = int(math.log2(lax.axis_size("dp")))
    upward = tuple(range(bits))
    downward = tuple(reversed(upward))

    def by_sequence(array):
        mine = lax.dynamic_index_in_dim(array, core, 0, False)
        theirs = lax.dynamic_index_in_dim(array, 1 - core, 0, False)
        return jnp.concatenate([mine, swapped(theirs)], axis=0)

    def by_rows(array):
        mine = array[:seq_dev]
        arrived = swapped(array[seq_dev:])
        return in_order(mine[None], arrived[None], core == 1, 0)

    sources = lax.rem(place - jnp.arange(count, dtype=jnp.int32) + count, count)
    slots = jnp.stack([2 * sources + core, 2 * sources + 1 - core], axis=1).reshape(-1)
    ranks = block_order[slots]

    rows_low = by_sequence(hidden)
    other_qkv = swapped(w_qkv)
    other_proj = swapped(w_proj)
    grad_low = by_sequence(cotangent)
    grad_rows = jnp.concatenate([grad_low, swapped(grad_low)], axis=0)
    grad_rows_near = lax.ppermute(grad_rows, "dp", pair_hops("dp", 0))
    grad_act = contract(w_down, grad_rows, 1, 1)

    inputs = wide(rows_low)
    normed, norm_one_pull = jax.vjp(layer_norm, inputs, wide(ln1_gain), wide(ln1_bias))
    normed_low = normed.astype(low_type)
    normed_own = part_of(normed_low, core, half_width, 1)
    normed_other = part_of(normed_low, 1 - core, half_width, 1)
    mixed = contract(w_qkv, normed_own, 0, 1) + contract(other_qkv, normed_other, 0, 1)
    offsets = jnp.concatenate([wide(q_bias), jnp.zeros((width,), full_type), wide(v_bias)])
    scales = jnp.concatenate([jnp.full((width,), scale, full_type), jnp.ones((2 * width,), full_type)])
    mixed = ((mixed + offsets[:, None]) * scales[:, None]).astype(low_type)

    def own_half(array):
        return part_of(array, core, half_width, 1) + swapped(
            part_of(array, 1 - core, half_width, 1)
        )

    def to_heads(array):
        array = array.reshape(-1, HEADS, depth, rows)
        array = jnp.pad(array, ((0, 0), (0, padded - HEADS), (0, 0), (0, 0)))
        array = array.reshape(-1, count, group, depth, rows)
        return jnp.transpose(array, (1, 0, 2, 3, 4))

    def from_heads(array):
        array = array.reshape(-1, padded, depth, rows)
        return array[:, :HEADS].reshape(-1, rows)

    normed_near = swapped(normed_other)
    mixed_heads, grad_act, grad_rows_near, normed_near = tied(
        scattered(to_heads(mixed)), grad_act, grad_rows_near, normed_near
    )
    out_heads, lse = attention_forward(ranks, mixed_heads)
    attended = from_heads(assembled([sent_back(out_heads)], ((0, group),)))
    attended_own = part_of(attended, core, half_width)
    attended_other = part_of(attended, 1 - core, half_width)
    branch = contract(attended_own, w_proj, 0, 0) + contract(attended_other, other_proj, 0, 0)
    middle = inputs + branch + wide(proj_bias)

    normed_two, norm_two_pull = jax.vjp(layer_norm, middle, wide(ln2_gain), wide(ln2_bias))
    normed_two_low, attended_near = tied(normed_two.astype(low_type), swapped(attended_other))
    rows_two = jnp.concatenate([normed_two_low, swapped(normed_two_low)], axis=0)
    low_high, top_high = bit_of("dp", 0), bit_of("dp", bits - 1)
    half_units = w_down.shape[0] // 2
    pre_act = contract(w_up, rows_two, 0, 1) + wide(up_bias)[:, None]
    activated, gelu_pull = jax.vjp(gelu_tanh, pre_act)
    act_low = row_major(activated.astype(low_type))
    act_near = lax.ppermute(part_of(act_low, 1 - low_high, half_units), "dp", pair_hops("dp", 0))
    grad_pre = row_major(gelu_pull(grad_act)[0].astype(low_type))
    up_send = jnp.concatenate([rows_two.T, part_of(grad_pre, 1 - top_high, half_units)])
    up_send, grad_pre = tied(up_send, grad_pre)
    up_near = lax.ppermute(up_send, "dp", pair_hops("dp", bits - 1))
    grad_up_bias = jnp.sum(wide(grad_pre), axis=1)

    back_terms = contract(grad_pre, w_up, 0, 1)
    grad_norm_two = back_terms[:rows] + wide(swapped(back_terms[rows:].astype(low_type)))
    grad_out = wide(grad_low)
    grad_down_bias = jnp.sum(grad_out, axis=0)
    grad_mid_norm, grad_ln2_gain, grad_ln2_bias = norm_two_pull(grad_norm_two)
    grad_mid = grad_out + grad_mid_norm
    grad_branch = grad_mid.astype(low_type)
    grad_proj_bias = jnp.sum(wide(grad_branch), axis=0)
    grad_attended = in_order(
        contract(w_proj, grad_branch, 1, 1).astype(low_type),
        contract(other_proj, grad_branch, 1, 1).astype(low_type),
        core == 1,
        0,
    )
    grad_heads = scattered(to_heads(grad_attended))[:, 0]
    branch_near = swapped(grad_branch)

    grad_w_down = contract(grad_rows, part_of(act_low, low_high, half_units), 0, 1) + contract(
        grad_rows_near, act_near, 0, 1
    )
    grad_heads, grad_w_down, branch_near = tied(
        grad_heads, row_major(grad_w_down.astype(low_type)), branch_near
    )
    down_share = reduced(grad_w_down, "dp", upward[1:])

    cut = (group + 1) // 2
    parts = ((0, cut), (cut, group)) if cut < group else ((0, group),)
    grads_of = [
        attention_backward(ranks, mixed_heads, out_heads, grad_heads, lse, part) for part in parts
    ]
    grads_of[0], grad_pre_late = tied(grads_of[0], grad_pre)
    grad_w_up = contract(rows_two, part_of(grad_pre_late, top_high, half_units), 0, 1) + contract(
        up_near[:width], up_near[width:], 1, 1
    )
    grad_w_up = row_major(grad_w_up.astype(low_type))
    backs = [sent_back(grads_of[0])]
    for later in grads_of[1:]:
        backs[-1], later, grad_w_up, branch_late, down_share = tied(
            backs[-1], later, grad_w_up, grad_branch, down_share
        )
        backs.append(sent_back(later))
    turns = int(math.log2(count))
    down_share = reduced(down_share, "ctx", range(turns - 1))
    up_share = reduced(grad_w_up, "dp", downward[1:])
    attended_both = jnp.concatenate([attended_own, attended_near], axis=1)
    branch_both = jnp.concatenate([grad_branch if cut == group else branch_late, branch_near])
    grad_w_proj = contract(attended_both, branch_both, 1, 0)
    grad_mixed, up_share, grad_w_proj, down_share = tied(
        from_heads(assembled(backs, parts)), up_share, grad_w_proj, down_share
    )
    query_rows = lax.broadcasted_iota(jnp.int32, (3 * width, 1), 0) < width
    grad_mixed = jnp.where(query_rows, grad_mixed * low_type(scale), grad_mixed)
    grad_mixed_sums = jnp.sum(wide(grad_mixed), axis=1)

    small_early = own_half(
        jnp.stack(
            [
                grad_mixed_sums[:width],
                grad_mixed_sums[2 * width :],
                grad_proj_bias,
                grad_ln2_gain,
                grad_ln2_bias,
                grad_down_bias,
            ]
        )
    )
    wide_rows = -(-grad_up_bias.shape[0] // half_width)
    up_bias_rows = jnp.pad(grad_up_bias, (0, wide_rows * half_width - grad_up_bias.shape[0]))
    small_early = jnp.concatenate([small_early, up_bias_rows.reshape(wide_rows, half_width)])

    normed_both = jnp.concatenate([normed_own, normed_near], axis=0)
    grad_mixed_both = jnp.concatenate([grad_mixed, swapped(grad_mixed)], axis=1)
    grad_w_qkv = contract(normed_both, grad_mixed_both, 0, 1)

    first = row_major(grad_w_qkv[:, : 2 * width].astype(low_type))
    second = row_major(
        jnp.concatenate([grad_w_qkv[:, 2 * width :], grad_w_proj], axis=1).astype(low_type)
    )
    half = down_share.shape[0] // 2
    high = bit_of("ctx", turns - 1)
    down_kept = part_of(down_share, high, half)
    down_near = lax.ppermute(
        part_of(down_share, 1 - high, half), "ctx", pair_hops("ctx", turns - 1)
    )
    first, second, up_share, down_kept, down_near = tied(
        first, second, up_share, down_kept, down_near
    )
    down_share = (wide(down_kept) + wide(down_near)).astype(low_type)

    first, second = reduced(first, "dp", upward[:1]), reduced(second, "dp", downward[:1])
    up_share = reduced(up_share, "ctx", range(1))
    down_share = spread(down_share, "ctx", range(1, turns)[::-1])
    first, second, up_share, down_share, act_late, small_late = tied(
        first, second, up_share, down_share, act_low, small_early
    )

    down_terms = contract(act_late, w_down, 0, 0)
    mlp_sum = down_terms[:rows] + wide(swapped(down_terms[rows:].astype(low_type)))
    output = by_rows((middle + mlp_sum + wide(down_bias)).astype(low_type))

    down_dims = (1,) + (0,) * (bits - 1)
    up_dims = (0,) * (bits - 1) + (1,)
    first, second = reduced(first, "dp", upward[1:]), reduced(second, "dp", downward[1:])
    up_share = reduced(up_share, "ctx", range(1, turns))
    down_share = spread(down_share, "ctx", range(1))
    first, second, up_share, down_share, output, grad_mixed = tied(
        first, second, up_share, down_share, output, grad_mixed
    )

    last = jnp.concatenate([first, second])
    sliced = last.shape[0] % count == 0
    down_parts = spread_both(in_two(down_share), down_dims, 0)
    up_share = spread(up_share, "ctx", range(1, turns)[::-1])
    last = reduced(last, "ctx", range(1)) if sliced else lax.psum(last, "ctx")
    grad_norm_one = in_order(
        contract(grad_mixed, w_qkv, 0, 1), contract(grad_mixed, other_qkv, 0, 1), core == 1, 1
    )
    down_parts, up_share, last, grad_norm_one, small_late = tied(
        down_parts, up_share, last, grad_norm_one, small_late
    )

    down_parts = spread_both(down_parts, down_dims, 1)
    up_share = spread(up_share, "ctx", range(1))
    last = reduced(last, "ctx", range(1, turns)) if sliced else last
    grad_in_norm, grad_ln1_gain, grad_ln1_bias = norm_one_pull(grad_norm_one)
    grad_hidden = by_rows((grad_mid + grad_in_norm).astype(low_type))
    small = jnp.concatenate([own_half(jnp.stack([grad_ln1_gain, grad_ln1_bias])), small_late])
    down_parts, up_share, last, small, grad_hidden = tied(
        down_parts, up_share, last, small, grad_hidden
    )

    down_total = wide(joined(down_parts, bits - 1)).T
    up_parts = spread_both(in_two(up_share), up_dims, 0)
    last = spread(last, "ctx", range(1, turns)[::-1]) if sliced else last
    small = summed(small, "dp", upward[:1])
    up_parts, last, small = tied(up_parts, last, small)

    up_parts = spread_both(up_parts, up_dims, 1)
    last = spread(last, "ctx", range(1)) if sliced else last
    small = summed(small, "dp", upward[1:])
    up_parts, last, small, down_total = tied(up_parts, last, small, down_total)

    up_total = wide(joined(up_parts, bits - 1))
    first, second = in_two(last)
    first, second = spread(first, "dp", downward[:1]), spread(second, "dp", upward[:1])
    small = summed(small, "ctx", range(1))
    first, second, small, up_total = tied(first, second, small, up_total)

    small_total = summed(small, "ctx", range(1, turns))
    first, second = spread(first, "dp", downward[1:]), spread(second, "dp", upward[1:])
    qkv_total = jnp.concatenate([wide(first), wide(second[:, :width])], axis=1)
    proj_total = wide(second[:, width:])
    up_bias_total = small_total[8:].reshape(-1)[: grad_up_bias.shape[0]]
    return (
        output,
        grad_hidden,
        small_total[0],
        small_total[1],
        qkv_total,
        small_total[2],
        small_total[3],
        proj_total,
        small_total[4],
        small_total[5],
        small_total[6],
        up_total,
        up_bias_total,
        down_total,
        small_total[7],
    )


def solution(mesh):
    placed = (
        P("dp", ("ctx", "wt"), None),
        P(),
        P(),
        P(),
        P("wt", None),
        P(),
        P(),
        P("wt", None),
        P(),
        P(),
        P(),
        P(None, "wt"),
        P("wt"),
        P("wt", None),
        P(),
        P("dp", ("ctx", "wt"), None),
    )
    return jax.shard_map(
        local,
        mesh=mesh,
        in_specs=placed,
        out_specs=(
            P("dp", ("ctx", "wt"), None),
            P("dp", ("ctx", "wt"), None),
            P("wt"),
            P("wt"),
            P("wt", None),
            P("wt"),
            P("wt"),
            P("wt", None),
            P("wt"),
            P("wt"),
            P("wt"),
            P(None, "wt"),
            P("wt"),
            P("wt", None),
            P("wt"),
        ),
        check_vma=False,
    )
```

```python
import math

import jax
import jax.numpy as jnp
from jax import lax
from jax.experimental import pallas as pl
from jax.experimental.layout import Layout, with_layout_constraint
from jax.experimental.pallas import tpu as pltpu
from jax.sharding import PartitionSpec as P

HEADS = 17

epsilon = 1e-05
masked_value = -1e30
low_type = jnp.bfloat16
full_type = jnp.float32


def wide(array):
    return array.astype(full_type)


def layer_norm(values, gain, offset):
    average = jnp.mean(values, axis=-1, keepdims=True)
    shifted = values - average
    variance = jnp.mean(shifted * shifted, axis=-1, keepdims=True)
    return shifted * lax.rsqrt(variance + epsilon) * gain + offset


def gelu_tanh(values):
    return jax.nn.gelu(values, approximate=True)


def contract(first, second, first_dim, second_dim):
    return lax.dot_general(
        first, second, (((first_dim,), (second_dim,)), ((), ())), preferred_element_type=full_type
    )


def repeat(start, stop, body, carry):
    if isinstance(start, int) and isinstance(stop, int) and stop - start <= 4:
        for index in range(start, stop):
            carry = body(index, carry)
        return carry
    return lax.fori_loop(start, stop, body, carry)


def pair_of(ref, index):
    return jnp.concatenate([ref[2 * index], ref[2 * index + 1]], axis=-1)


def put_pair(ref, index, tile):
    half = tile.shape[-1] // 2
    ref[2 * index] = tile[:, :half].astype(ref.dtype)
    ref[2 * index + 1] = tile[:, half:].astype(ref.dtype)


def causal(scores):
    key_at = lax.broadcasted_iota(jnp.int32, scores.shape, 0)
    query_at = lax.broadcasted_iota(jnp.int32, scores.shape, 1)
    return jnp.where(key_at <= query_at, scores, masked_value)


def forward_kernel(ranks, mixed_ref, out_ref, lse_ref, queries, keys, values, outs):
    count = mixed_ref.shape[0]
    block = mixed_ref.shape[-1] // 2
    for piece in range(count):
        for half in range(2):
            rank = ranks[2 * piece + half]
            span = slice(half * block, (half + 1) * block)
            queries[rank] = mixed_ref[piece, 0, 0, :, span]
            keys[rank] = mixed_ref[piece, 1, 0, :, span]
            values[rank] = mixed_ref[piece, 2, 0, :, span]

    def query_tile(at, unused):
        query = pair_of(queries, at)

        def scores_at(key_at, diagonal=False):
            scores = contract(pair_of(keys, key_at), query, 0, 0)
            return causal(scores) if diagonal else scores

        def key_tile(key_at, carry, diagonal=False):
            highest, total, accum = carry
            scores = scores_at(key_at, diagonal)
            new_highest = jnp.maximum(highest, jnp.max(scores, axis=0, keepdims=True))
            probs = jnp.exp(scores - new_highest)
            shrink = jnp.exp(highest - new_highest)
            total = total * shrink + jnp.sum(probs, axis=0, keepdims=True)
            accum = accum * shrink + contract(
                pair_of(values, key_at), probs.astype(low_type), 1, 0
            )
            return new_highest, total, accum

        if isinstance(at, int):
            tiles = [scores_at(key_at, key_at == at) for key_at in range(at + 1)]
            highest = jnp.max(tiles[0], axis=0, keepdims=True)
            for tile in tiles[1:]:
                highest = jnp.maximum(highest, jnp.max(tile, axis=0, keepdims=True))
            total = jnp.zeros((1, 2 * block), full_type)
            accum = jnp.zeros(query.shape, full_type)
            for key_at, tile in enumerate(tiles):
                probs = jnp.exp(tile - highest)
                total = total + jnp.sum(probs, axis=0, keepdims=True)
                accum = accum + contract(pair_of(values, key_at), probs.astype(low_type), 1, 0)
        else:
            start = (
                jnp.full((1, 2 * block), masked_value, full_type),
                jnp.zeros((1, 2 * block), full_type),
                jnp.zeros(query.shape, full_type),
            )
            carry = lax.fori_loop(0, at, key_tile, start)
            highest, total, accum = key_tile(at, carry, True)
        put_pair(outs, at, accum / total)
        lse_ref[0, pl.ds(at, 1), :] = highest + jnp.log(total)
        return unused

    repeat(0, count, query_tile, 0)
    for piece in range(count):
        for half in range(2):
            rank = ranks[2 * piece + half]
            out_ref[piece, 0, :, half * block : (half + 1) * block] = outs[rank]


def backward_kernel(
    ranks,
    mixed_ref,
    out_ref,
    grad_ref,
    lse_ref,
    result_ref,
    queries,
    keys,
    values,
    outs,
    grads,
    query_grads,
    key_grads,
    value_grads,
    deltas,
):
    count = mixed_ref.shape[0]
    block = mixed_ref.shape[-1] // 2
    for piece in range(count):
        for half in range(2):
            rank = ranks[2 * piece + half]
            span = slice(half * block, (half + 1) * block)
            queries[rank] = mixed_ref[piece, 0, 0, :, span]
            keys[rank] = mixed_ref[piece, 1, 0, :, span]
            values[rank] = mixed_ref[piece, 2, 0, :, span]
            outs[rank] = out_ref[piece, 0, :, span]
            grads[rank] = grad_ref[piece, 0, :, span]

    def delta_tile(at, unused):
        terms = pair_of(outs, at).astype(full_type) * pair_of(grads, at).astype(full_type)
        deltas[pl.ds(at, 1), :] = jnp.sum(terms, axis=0, keepdims=True)
        zeros = jnp.zeros(query_grads.shape[1:], full_type)
        query_grads[2 * at] = zeros
        query_grads[2 * at + 1] = zeros
        return unused

    repeat(0, count, delta_tile, 0)

    def key_tile(key_at, unused):
        key = pair_of(keys, key_at)
        value = pair_of(values, key_at)

        def query_tile(at, carry, diagonal=False):
            key_grad, value_grad = carry
            query = pair_of(queries, at)
            grad = pair_of(grads, at)
            scores = contract(key, query, 0, 0)
            if diagonal:
                scores = causal(scores)
            probs = jnp.exp(scores - lse_ref[0, pl.ds(at, 1), :])
            grad_probs = contract(value, grad, 0, 0)
            grad_scores = (probs * (grad_probs - deltas[pl.ds(at, 1), :])).astype(low_type)
            value_grad = value_grad + contract(grad, probs.astype(low_type), 1, 1)
            key_grad = key_grad + contract(query, grad_scores, 1, 1)
            query_grad = contract(key, grad_scores, 1, 0)
            query_grads[2 * at] += query_grad[:, :block]
            query_grads[2 * at + 1] += query_grad[:, block:]
            return key_grad, value_grad

        start = (jnp.zeros(key.shape, full_type), jnp.zeros(key.shape, full_type))
        carry = query_tile(key_at, start, True)
        key_grad, value_grad = repeat(key_at + 1, count, query_tile, carry)
        put_pair(key_grads, key_at, key_grad)
        put_pair(value_grads, key_at, value_grad)
        return unused

    repeat(0, count, key_tile, 0)
    for piece in range(count):
        for half in range(2):
            rank = ranks[2 * piece + half]
            span = slice(half * block, (half + 1) * block)
            result_ref[piece, 0, 0, :, span] = query_grads[rank].astype(low_type)
            result_ref[piece, 1, 0, :, span] = key_grads[rank]
            result_ref[piece, 2, 0, :, span] = value_grads[rank]


def attention_forward(ranks, mixed):
    count, _, heads, depth, rows = mixed.shape
    blocks = (2 * count, depth, rows // 2)
    return pl.pallas_call(
        forward_kernel,
        out_shape=(
            jax.ShapeDtypeStruct((count, heads, depth, rows), low_type),
            jax.ShapeDtypeStruct((heads, count, rows), full_type),
        ),
        grid_spec=pltpu.PrefetchScalarGridSpec(
            num_scalar_prefetch=1,
            grid=(heads,),
            in_specs=[
                pl.BlockSpec((count, 3, 1, depth, rows), lambda head, _: (0, 0, head, 0, 0))
            ],
            out_specs=(
                pl.BlockSpec((count, 1, depth, rows), lambda head, _: (0, head, 0, 0)),
                pl.BlockSpec((1, count, rows), lambda head, _: (head, 0, 0)),
            ),
            scratch_shapes=[pltpu.VMEM(blocks, low_type) for _ in range(4)],
        ),
        compiler_params=pltpu.CompilerParams(vmem_limit_bytes=40 * 2**20),
        cost_estimate=pl.CostEstimate(
            flops=2 * heads * count * (count + 1) * rows * rows * depth,
            bytes_accessed=8 * heads * count * depth * rows,
            transcendentals=heads * count * (count + 1) * rows * rows // 2,
        ),
    )(ranks, mixed)


def attention_backward(ranks, mixed, outs, grads, lse, part):
    count, _, _, depth, rows = mixed.shape
    start, stop = part
    blocks = (2 * count, depth, rows // 2)
    three_block = (count, 3, 1, depth, rows)
    three = pl.BlockSpec(three_block, lambda head, _: (0, 0, head + start, 0, 0))
    one = pl.BlockSpec((count, 1, depth, rows), lambda head, _: (0, head + start, 0, 0))
    return pl.pallas_call(
        backward_kernel,
        out_shape=jax.ShapeDtypeStruct((count, 3, stop - start, depth, rows), low_type),
        grid_spec=pltpu.PrefetchScalarGridSpec(
            num_scalar_prefetch=1,
            grid=(stop - start,),
            in_specs=[
                three,
                one,
                one,
                pl.BlockSpec((1, count, rows), lambda head, _: (head + start, 0, 0)),
            ],
            out_specs=pl.BlockSpec(three_block, lambda head, _: (0, 0, head, 0, 0)),
            scratch_shapes=[pltpu.VMEM(blocks, low_type) for _ in range(5)]
            + [pltpu.VMEM(blocks, full_type)]
            + [pltpu.VMEM(blocks, low_type) for _ in range(2)]
            + [pltpu.VMEM((count, rows), full_type)],
        ),
        compiler_params=pltpu.CompilerParams(vmem_limit_bytes=40 * 2**20),
        cost_estimate=pl.CostEstimate(flops=0, bytes_accessed=0, transcendentals=0),
    )(ranks, mixed, outs, grads, lse)


def swapped(array):
    return lax.ppermute(array, "wt", [(0, 1), (1, 0)])


def part_of(array, index, size, axis=0):
    return lax.dynamic_slice_in_dim(array, index * size, size, axis)


def in_order(first, second, flip, axis):
    return jnp.where(
        flip, jnp.concatenate([second, first], axis), jnp.concatenate([first, second], axis)
    )


def scattered(send):
    count = lax.axis_size("ctx")
    place = lax.axis_index("ctx")
    pieces = []
    for shift in range(count):
        piece = lax.dynamic_index_in_dim(send, lax.rem(place + shift, count), 0, False)
        if shift:
            hops = [(one, (one + shift) % count) for one in range(count)]
            piece = lax.ppermute(piece, "ctx", hops)
        pieces.append(piece)
    return jnp.stack(pieces)


def sent_back(pieces):
    count = lax.axis_size("ctx")
    back = [pieces[0]]
    for shift in range(1, count):
        hops = [(one, (one - shift) % count) for one in range(count)]
        back.append(lax.ppermute(pieces[shift], "ctx", hops))
    return back


def assembled(backs, parts):
    count = len(backs[0])
    lead, (depth, rows) = backs[0][0].shape[:-3], backs[0][0].shape[-2:]
    result = jnp.zeros((*lead, count, parts[-1][1], depth, rows), low_type)
    for back, (start, _) in zip(backs, parts):
        for shift, piece in enumerate(back):
            source = lax.rem(lax.axis_index("ctx") + shift, count)
            at = (0,) * len(lead) + (source, start, 0, 0)
            result = lax.dynamic_update_slice(result, jnp.expand_dims(piece, len(lead)), at)
    return result


def pair_hops(axis, bit):
    return [(one, one ^ (1 << bit)) for one in range(lax.axis_size(axis))]


def bit_of(axis, bit):
    return lax.rem(lax.div(lax.axis_index(axis), 1 << bit), 2)


def reduced(array, axis, order):
    for bit in order:
        half = array.shape[0] // 2
        high = bit_of(axis, bit)
        kept = part_of(array, high, half)
        arrived = lax.ppermute(part_of(array, 1 - high, half), axis, pair_hops(axis, bit))
        array = (wide(kept) + wide(arrived)).astype(low_type)
    return array


def spread(array, axis, order, dim=0):
    for bit in order:
        arrived = lax.ppermute(array, axis, pair_hops(axis, bit))
        array = in_order(array, arrived, bit_of(axis, bit) == 1, dim)
    return array


def spread_both(parts, dims, step):
    order = range(len(dims))
    return tuple(
        spread(part, "dp", (bits[step],), dims[bits[step]])
        for part, bits in zip(parts, (order, order[::-1]))
    )


def in_two(array):
    half = array.shape[0] // 2
    return array[:half], array[half:]


def joined(parts, bits):
    forth, back = parts
    forth = forth.reshape((2,) * bits + (-1, forth.shape[1]))
    forth = jnp.transpose(forth, (*reversed(range(bits)), bits, bits + 1))
    return jnp.stack([forth, back.reshape(forth.shape)], axis=bits).reshape(-1, forth.shape[-1])


def row_major(array):
    return with_layout_constraint(array, Layout(major_to_minor=(0, 1)))


def tied(*arrays):
    return lax.optimization_barrier(arrays)


def summed(array, axis, order):
    for bit in order:
        array = array + lax.ppermute(array, axis, pair_hops(axis, bit))
    return array


def local(
    hidden,
    block_order,
    ln1_gain,
    ln1_bias,
    w_qkv,
    q_bias,
    v_bias,
    w_proj,
    proj_bias,
    ln2_gain,
    ln2_bias,
    w_up,
    up_bias,
    w_down,
    down_bias,
    cotangent,
):
    seqs, seq_dev, width = hidden.shape
    depth = width // HEADS
    scale = 1.0 / math.sqrt(depth)
    count = lax.axis_size("ctx")
    place = lax.axis_index("ctx")
    core = lax.axis_index("wt")
    half_width = width // 2
    rows = 2 * seq_dev
    group = -(-HEADS // count)
    padded = group * count
    bits = int(math.log2(lax.axis_size("dp")))
    upward = tuple(range(bits))
    downward = tuple(reversed(upward))

    def by_sequence(array):
        mine = lax.dynamic_index_in_dim(array, core, 0, False)
        theirs = lax.dynamic_index_in_dim(array, 1 - core, 0, False)
        return jnp.concatenate([mine, swapped(theirs)], axis=0)

    def by_rows(array):
        mine = array[:seq_dev]
        arrived = swapped(array[seq_dev:])
        return in_order(mine[None], arrived[None], core == 1, 0)

    sources = lax.rem(place - jnp.arange(count, dtype=jnp.int32) + count, count)
    slots = jnp.stack([2 * sources + core, 2 * sources + 1 - core], axis=1).reshape(-1)
    ranks = block_order[slots]

    rows_low = by_sequence(hidden)
    other_qkv = swapped(w_qkv)
    other_proj = swapped(w_proj)
    grad_low = by_sequence(cotangent)
    grad_rows = jnp.concatenate([grad_low, swapped(grad_low)], axis=0)

    inputs = wide(rows_low)
    normed, norm_one_pull = jax.vjp(layer_norm, inputs, wide(ln1_gain), wide(ln1_bias))
    normed_low = normed.astype(low_type)
    normed_own = part_of(normed_low, core, half_width, 1)
    normed_other = part_of(normed_low, 1 - core, half_width, 1)
    mixed = contract(w_qkv, normed_own, 0, 1) + contract(other_qkv, normed_other, 0, 1)
    offsets = jnp.concatenate([wide(q_bias), jnp.zeros((width,), full_type), wide(v_bias)])
    scales = jnp.concatenate([jnp.full((width,), scale, full_type), jnp.ones((2 * width,), full_type)])
    mixed = ((mixed + offsets[:, None]) * scales[:, None]).astype(low_type)

    def own_half(array):
        return part_of(array, core, half_width, 1) + swapped(
            part_of(array, 1 - core, half_width, 1)
        )

    def to_heads(array):
        array = array.reshape(-1, HEADS, depth, rows)
        array = jnp.pad(array, ((0, 0), (0, padded - HEADS), (0, 0), (0, 0)))
        array = array.reshape(-1, count, group, depth, rows)
        return jnp.transpose(array, (1, 0, 2, 3, 4))

    def from_heads(array):
        array = array.reshape(-1, padded, depth, rows)
        return array[:, :HEADS].reshape(-1, rows)

    normed_near = swapped(normed_other)
    sends, grad_rows = tied(to_heads(mixed), grad_rows)
    grad_rows_near = lax.ppermute(grad_rows, "dp", pair_hops("dp", 0))
    grad_act = contract(w_down, grad_rows, 1, 1)
    mixed_heads, grad_act, grad_rows_near, normed_near = tied(
        scattered(sends), grad_act, grad_rows_near, normed_near
    )
    out_heads, lse = attention_forward(ranks, mixed_heads)
    attended = from_heads(assembled([sent_back(out_heads)], ((0, group),)))
    attended_own = part_of(attended, core, half_width)
    attended_other = part_of(attended, 1 - core, half_width)
    branch = contract(attended_own, w_proj, 0, 0) + contract(attended_other, other_proj, 0, 0)
    middle = inputs + branch + wide(proj_bias)

    normed_two, norm_two_pull = jax.vjp(layer_norm, middle, wide(ln2_gain), wide(ln2_bias))
    normed_two_low, attended_near = tied(normed_two.astype(low_type), swapped(attended_other))
    rows_two = jnp.concatenate([normed_two_low, swapped(normed_two_low)], axis=0)
    low_high, top_high = bit_of("dp", 0), bit_of("dp", bits - 1)
    half_units = w_down.shape[0] // 2
    pre_act = contract(w_up, rows_two, 0, 1) + wide(up_bias)[:, None]
    activated, gelu_pull = jax.vjp(gelu_tanh, pre_act)
    act_low = row_major(activated.astype(low_type))
    act_near = lax.ppermute(part_of(act_low, 1 - low_high, half_units), "dp", pair_hops("dp", 0))
    grad_pre = row_major(gelu_pull(grad_act)[0].astype(low_type))
    up_send = jnp.concatenate([rows_two.T, part_of(grad_pre, 1 - top_high, half_units)])
    up_send, grad_pre = tied(up_send, grad_pre)
    up_near = lax.ppermute(up_send, "dp", pair_hops("dp", bits - 1))
    grad_up_bias = jnp.sum(wide(grad_pre), axis=1)

    back_terms = contract(grad_pre, w_up, 0, 1)
    grad_norm_two = back_terms[:rows] + wide(swapped(back_terms[rows:].astype(low_type)))
    grad_out = wide(grad_low)
    grad_down_bias = jnp.sum(grad_out, axis=0)
    grad_mid_norm, grad_ln2_gain, grad_ln2_bias = norm_two_pull(grad_norm_two)
    grad_mid = grad_out + grad_mid_norm
    grad_branch = grad_mid.astype(low_type)
    grad_proj_bias = jnp.sum(wide(grad_branch), axis=0)
    grad_attended = in_order(
        contract(w_proj, grad_branch, 1, 1).astype(low_type),
        contract(other_proj, grad_branch, 1, 1).astype(low_type),
        core == 1,
        0,
    )
    grad_heads = scattered(to_heads(grad_attended))[:, 0]
    branch_near = swapped(grad_branch)

    grad_w_down = contract(grad_rows, part_of(act_low, low_high, half_units), 0, 1) + contract(
        grad_rows_near, act_near, 0, 1
    )
    grad_heads, grad_w_down, branch_near = tied(
        grad_heads, row_major(grad_w_down.astype(low_type)), branch_near
    )
    down_share = reduced(grad_w_down, "dp", upward[1:])

    cut = (group + 1) // 2
    parts = ((0, cut), (cut, group)) if cut < group else ((0, group),)
    grads_of = [
        attention_backward(ranks, mixed_heads, out_heads, grad_heads, lse, part) for part in parts
    ]
    grads_of[0], grad_pre_late = tied(grads_of[0], grad_pre)
    grad_w_up = contract(rows_two, part_of(grad_pre_late, top_high, half_units), 0, 1) + contract(
        up_near[:width], up_near[width:], 1, 1
    )
    grad_w_up = row_major(grad_w_up.astype(low_type))
    backs = [sent_back(grads_of[0])]
    for later in grads_of[1:]:
        backs[-1], later, grad_w_up, branch_late, down_share = tied(
            backs[-1], later, grad_w_up, grad_branch, down_share
        )
        backs.append(sent_back(later))
    turns = int(math.log2(count))
    down_share = reduced(down_share, "ctx", range(turns - 1))
    up_share = reduced(grad_w_up, "dp", downward[1:])
    attended_both = jnp.concatenate([attended_own, attended_near], axis=1)
    branch_both = jnp.concatenate([grad_branch if cut == group else branch_late, branch_near])
    grad_w_proj = contract(attended_both, branch_both, 1, 0)
    grad_mixed, up_share, grad_w_proj, down_share = tied(
        from_heads(assembled(backs, parts)), up_share, grad_w_proj, down_share
    )
    query_rows = lax.broadcasted_iota(jnp.int32, (3 * width, 1), 0) < width
    grad_mixed = jnp.where(query_rows, grad_mixed * low_type(scale), grad_mixed)
    grad_mixed_sums = jnp.sum(wide(grad_mixed), axis=1)

    small_early = own_half(
        jnp.stack(
            [
                grad_mixed_sums[:width],
                grad_mixed_sums[2 * width :],
                grad_proj_bias,
                grad_ln2_gain,
                grad_ln2_bias,
                grad_down_bias,
            ]
        )
    )
    wide_rows = -(-grad_up_bias.shape[0] // half_width)
    up_bias_rows = jnp.pad(grad_up_bias, (0, wide_rows * half_width - grad_up_bias.shape[0]))
    small_early = jnp.concatenate([small_early, up_bias_rows.reshape(wide_rows, half_width)])

    normed_both = jnp.concatenate([normed_own, normed_near], axis=0)
    grad_mixed_both = jnp.concatenate([grad_mixed, swapped(grad_mixed)], axis=1)
    grad_w_qkv = contract(normed_both, grad_mixed_both, 0, 1)

    first = row_major(grad_w_qkv[:, : 2 * width].astype(low_type))
    second = row_major(
        jnp.concatenate([grad_w_qkv[:, 2 * width :], grad_w_proj], axis=1).astype(low_type)
    )
    half = down_share.shape[0] // 2
    high = bit_of("ctx", turns - 1)
    down_kept = part_of(down_share, high, half)
    down_near = lax.ppermute(
        part_of(down_share, 1 - high, half), "ctx", pair_hops("ctx", turns - 1)
    )
    first, second, up_share, down_kept, down_near = tied(
        first, second, up_share, down_kept, down_near
    )
    down_share = (wide(down_kept) + wide(down_near)).astype(low_type)

    first, second = reduced(first, "dp", upward[:1]), reduced(second, "dp", downward[:1])
    up_share = reduced(up_share, "ctx", range(1))
    down_share = spread(down_share, "ctx", range(1, turns)[::-1])
    first, second, up_share, down_share, act_late, small_late = tied(
        first, second, up_share, down_share, act_low, small_early
    )

    down_terms = contract(act_late, w_down, 0, 0)
    mlp_sum = down_terms[:rows] + wide(swapped(down_terms[rows:].astype(low_type)))
    output = by_rows((middle + mlp_sum + wide(down_bias)).astype(low_type))

    down_dims = (1,) + (0,) * (bits - 1)
    up_dims = (0,) * (bits - 1) + (1,)
    first, second = reduced(first, "dp", upward[1:]), reduced(second, "dp", downward[1:])
    up_share = reduced(up_share, "ctx", range(1, turns))
    down_share = spread(down_share, "ctx", range(1))
    first, second, up_share, down_share, output, grad_mixed = tied(
        first, second, up_share, down_share, output, grad_mixed
    )

    last = jnp.concatenate([first, second])
    sliced = last.shape[0] % count == 0
    down_parts = spread_both(in_two(down_share), down_dims, 0)
    up_share = spread(up_share, "ctx", range(1, turns)[::-1])
    last = reduced(last, "ctx", range(1)) if sliced else lax.psum(last, "ctx")
    grad_norm_one = in_order(
        contract(grad_mixed, w_qkv, 0, 1), contract(grad_mixed, other_qkv, 0, 1), core == 1, 1
    )
    down_parts, up_share, last, grad_norm_one, small_late = tied(
        down_parts, up_share, last, grad_norm_one, small_late
    )

    down_parts = spread_both(down_parts, down_dims, 1)
    up_share = spread(up_share, "ctx", range(1))
    last = reduced(last, "ctx", range(1, turns)) if sliced else last
    grad_in_norm, grad_ln1_gain, grad_ln1_bias = norm_one_pull(grad_norm_one)
    grad_hidden = by_rows((grad_mid + grad_in_norm).astype(low_type))
    small = jnp.concatenate([own_half(jnp.stack([grad_ln1_gain, grad_ln1_bias])), small_late])
    down_parts, up_share, last, small, grad_hidden = tied(
        down_parts, up_share, last, small, grad_hidden
    )

    down_total = wide(joined(down_parts, bits - 1)).T
    up_parts = spread_both(in_two(up_share), up_dims, 0)
    last = spread(last, "ctx", range(1, turns)[::-1]) if sliced else last
    small = summed(small, "dp", upward[:1])
    up_parts, last, small = tied(up_parts, last, small)

    up_parts = spread_both(up_parts, up_dims, 1)
    last = spread(last, "ctx", range(1)) if sliced else last
    small = summed(small, "dp", upward[1:])
    up_parts, last, small, down_total = tied(up_parts, last, small, down_total)

    up_total = wide(joined(up_parts, bits - 1))
    first, second = in_two(last)
    first, second = spread(first, "dp", downward[:1]), spread(second, "dp", upward[:1])
    small = summed(small, "ctx", range(1))
    first, second, small, up_total = tied(first, second, small, up_total)

    small_total = summed(small, "ctx", range(1, turns))
    first, second = spread(first, "dp", downward[1:-1]), spread(second, "dp", upward[1:-1])
    size = first.shape[0]
    qkv_total = jnp.zeros((2 * size, 3 * width), full_type)
    proj_total = jnp.zeros((2 * size, width), full_type)
    for near in (False, True):
        ends = []
        for part, bit in ((first, downward[-1]), (second, upward[-1])):
            high = bit_of("dp", bit)
            if near:
                part = lax.ppermute(part, "dp", pair_hops("dp", bit))
                high = 1 - high
            ends.append((wide(part), high * size))
        (one, one_at), (two, two_at) = ends
        qkv_total = lax.dynamic_update_slice(qkv_total, one, (one_at, 0))
        qkv_total = lax.dynamic_update_slice(qkv_total, two[:, :width], (two_at, 2 * width))
        proj_total = lax.dynamic_update_slice(proj_total, two[:, width:], (two_at, 0))
    up_bias_total = small_total[8:].reshape(-1)[: grad_up_bias.shape[0]]
    return (
        output,
        grad_hidden,
        small_total[0],
        small_total[1],
        qkv_total,
        small_total[2],
        small_total[3],
        proj_total,
        small_total[4],
        small_total[5],
        small_total[6],
        up_total,
        up_bias_total,
        down_total,
        small_total[7],
    )


def solution(mesh):
    placed = (
        P("dp", ("ctx", "wt"), None),
        P(),
        P(),
        P(),
        P("wt", None),
        P(),
        P(),
        P("wt", None),
        P(),
        P(),
        P(),
        P(None, "wt"),
        P("wt"),
        P("wt", None),
        P(),
        P("dp", ("ctx", "wt"), None),
    )
    return jax.shard_map(
        local,
        mesh=mesh,
        in_specs=placed,
        out_specs=(
            P("dp", ("ctx", "wt"), None),
            P("dp", ("ctx", "wt"), None),
            P("wt"),
            P("wt"),
            P("wt", None),
            P("wt"),
            P("wt"),
            P("wt", None),
            P("wt"),
            P("wt"),
            P("wt"),
            P(None, "wt"),
            P("wt"),
            P("wt", None),
            P("wt"),
        ),
        check_vma=False,
    )
```
